256 devices in a mesh: dp: 4 (over y), mp: 64 (over x, z, core).
Axes of the slice: x: 4, y: 4, z: 8, core: 2. Of those that a mesh axis runs over, the one named last changes fastest.
Arguments:
- grad_parts: bfloat16 [4, 2, 16384, 8192], P('dp', None, 'mp'), may hold values from -9 to 9
- omega: bfloat16 [8192, 512], P('dp'), may hold values from -0.0625 to 0.0625
- first_moment: float32 [512, 2, 8192], P('mp', None, 'dp'), may hold values from -0.75 to 0.75
- second_moment: float32 [512, 2, 8192], P('mp', None, 'dp'), may hold values from 0.0005 to 0.02
Outputs:
- new_first: float32 [512, 2, 8192], P('mp', None, 'dp')
- new_second: float32 [512, 2, 8192], P('mp', None, 'dp')
- weight_delta: bfloat16 [2, 16384, 8192], P(None, 'mp', 'dp')
The draws below stay inside these ranges and needn't reach their ends.
All inputs are finite; a program needn't handle non-finite values.
Results may differ from the reference program's by a relative error of at most 0.03.
Values may be sent and summed in bfloat16 or wider, within the bound.
A program may use at most 128 MiB of HBM per device.

```python
import math
import jax
import jax.numpy as jnp
from jax import lax

D = 8192
HID = 16384
RANK = 512
LAYERS = 2
N_DP = 4
N_MP = 64


def draw_grad_parts(key, part):
    key = jax.random.fold_in(key, 11)
    key_block, key_row, key_entry, key_order, key_rough = jax.random.split(key, 5)
    block_level = jax.random.uniform(key_block, (LAYERS, N_MP), jnp.float32)
    block_scale = jnp.power(10.0, block_level - 0.5)
    row_scale = jnp.repeat(block_scale, HID // N_MP, axis=1)
    row_level = jax.random.uniform(key_row, (LAYERS, HID), jnp.float32)
    row_scale = row_scale * jnp.power(2.0, row_level) / 1.42
    orders = jnp.stack([jax.random.permutation(jax.random.fold_in(key_order, layer_index), D) for layer_index in range(LAYERS)])
    leading = RANK // 4
    decayed = jnp.power(10.0, -orders.astype(jnp.float32) / leading)
    column_scale = jnp.where(orders < leading, decayed, 0.04)
    column_scale = column_scale * (1.0 + jax.random.uniform(key_rough, (LAYERS, D), jnp.float32)) / 2.0
    full_shape = (N_DP, LAYERS, HID, D)
    entries = jnp.clip(0.5 * jax.random.normal(key_entry, full_shape, jnp.float32), -2.0, 2.0)
    values = entries * row_scale[None, :, :, None] * column_scale[None, :, None, :]
    return values.astype(jnp.bfloat16)


def block_levels(key, extent, cuts, least, top_value):
    factor_of, own = 1.0, jax.random.fold_in(key, 6)
    for dim, blocks in cuts:
        heights = jnp.exp(jax.random.uniform(jax.random.fold_in(own, dim), (blocks,), jnp.float32, least / len(cuts), top_value / len(cuts)))
        factor_of = factor_of * jnp.repeat(heights, extent[dim] // blocks).reshape([-1 if axis == dim else 1 for axis in range(len(extent))])
    return factor_of


def bell_draw(key, shape, scale, bound, cuts=(), kind=jnp.bfloat16):
    drawn = scale * jax.random.normal(key, shape, jnp.float32)
    if cuts:
        drawn = drawn * block_levels(key, shape, cuts, -0.22, 0.18)
    return jnp.clip(drawn, -bound, bound).astype(kind)


def setup_inputs(seed: int = 0) -> dict:
    seeds = jax.random.split(jax.random.key(seed), 5)
    return {
        "grad_parts": draw_grad_parts(jax.random.fold_in(seeds[4], 71), 0),
        "omega": bell_draw(seeds[1], (D, RANK), D ** -0.5, 0.0625, ((0, 4),)),
        "first_moment": bell_draw(seeds[2], (RANK, LAYERS, D), 0.05, 0.75, ((0, 64), (2, 4)), jnp.float32),
        "second_moment": jnp.clip(jnp.exp(math.log(0.02) - 3.6888794 * jax.random.uniform(seeds[3], (RANK, LAYERS, D), jnp.float32) ** block_levels(seeds[3], (RANK, LAYERS, D), ((0, 64), (2, 4)), -0.2, 0.2)), 0.0005, 0.02),
    }


def reference(grad_parts, omega, first_moment, second_moment):
    firsts = []
    seconds = []
    deltas = []
    for layer_index in range(LAYERS):
        total = grad_parts[0, layer_index].astype(jnp.float32)
        for part_index in range(1, N_DP):
            total = total + grad_parts[part_index, layer_index].astype(jnp.float32)
        summed = total.astype(jnp.bfloat16)
        panel = jnp.dot(summed.astype(jnp.float32), omega.astype(jnp.float32), preferred_element_type=jnp.float32)
        gram = jnp.dot(panel.T, panel, precision=lax.Precision.HIGHEST)
        lower = jnp.linalg.cholesky(gram)
        basis = lax.linalg.triangular_solve(lower, panel, left_side=False, lower=True, transpose_a=True)
        basis = basis.astype(jnp.bfloat16)
        projected = jnp.dot(basis.T.astype(jnp.float32), summed.astype(jnp.float32), preferred_element_type=jnp.float32)
        fresh_first = 0.9 * first_moment[:, layer_index] + 0.1 * projected
        fresh_second = 0.999 * second_moment[:, layer_index] + 0.001 * projected * projected
        normalized = (fresh_first / (jnp.sqrt(fresh_second) + 1e-08)).astype(jnp.bfloat16)
        delta = jnp.dot(basis.astype(jnp.float32), normalized.astype(jnp.float32), preferred_element_type=jnp.float32).astype(jnp.bfloat16)
        firsts.append(fresh_first)
        seconds.append(fresh_second)
        deltas.append(delta)
    return (jnp.stack(firsts, axis=1), jnp.stack(seconds, axis=1), jnp.stack(deltas, axis=0))
```

```python
import functools

import jax
import jax.numpy as jnp
from jax import lax
from jax.experimental import pallas as pl
from jax.experimental.pallas import tpu as pltpu
from jax.sharding import PartitionSpec as P

HIGHEST = lax.Precision.HIGHEST
MESH = pl.DeviceIdType.MESH
NT = (((1,), (1,)), ((), ()))
TN = (((0,), (0,)), ((), ()))
BF = jnp.bfloat16
F32 = jnp.float32

LAYERS = 2
ROWS = 256
D = 8192
OWN = 2048
HALF = 1024
RANK = 512
B = 128
NY, NX, NZ, NC = 4, 4, 8, 2


def place():
    mp = lax.axis_index("mp")
    return lax.axis_index("dp"), mp // (NZ * NC), (mp // NC) % NZ, mp % NC


def device(y, x, z, c):
    return {"dp": y, "mp": x * (NZ * NC) + z * NC + c}


def greet(peers):
    barrier = pltpu.get_barrier_semaphore()
    for peer in peers:
        pl.semaphore_signal(barrier, inc=1, device_id=peer, device_id_type=MESH)
    pl.semaphore_wait(barrier, len(peers))


def along(axis, spot, k):
    y, x, z, c = spot
    if axis == "y":
        return device((y + k) % NY, x, z, c)
    if axis == "x":
        return device(y, (x + k) % NX, z, c)
    if axis == "z":
        return device(y, x, (z + k) % NZ, c)
    return device(y, x, z, 1 - c)


def ship(src, dst, send, recv, peer):
    copy = pltpu.make_async_remote_copy(
        src_ref=src, dst_ref=dst, send_sem=send, recv_sem=recv, device_id=peer, device_id_type=MESH
    )
    copy.start()
    return copy


def span(start, size):
    return pl.ds(pl.multiple_of(start, size), size)


def gram_kernel(part_ref, panel_ref, blocks_ref, rs_buf, mine, core_buf, chip, z_buf, strip, x_buf, sems):
    spot = place()
    y, x, z, c = spot
    peers = [along("y", spot, k) for k in range(1, NY)]
    peers += [along("z", spot, k) for k in range(1, NZ)]
    peers += [along("x", spot, k) for k in range(1, NX)]
    peers += [along("c", spot, 1)]
    greet(peers)
    done = []
    count = [0]

    def go(src, dst, peer):
        copy = ship(src, dst, sems.at[0, count[0]], sems.at[1, count[0]], peer)
        count[0] += 1
        done.append(copy)
        return copy

    q = ROWS // NY
    own = span(y * q, q)
    copies = [
        go(part_ref.at[:, span(((y + k) % NY) * q, q), :], rs_buf.at[k - 1], along("y", spot, k)) for k in range(1, NY)
    ]
    total = part_ref[:, own, :].astype(F32)
    for k, copy in enumerate(copies):
        copy.wait_recv()
        total = total + rs_buf[k].astype(F32)
    panel_ref[:, own, :] = total.astype(BF)
    copies = [go(panel_ref.at[:, own, :], panel_ref.at[:, own, :], along("y", spot, k)) for k in range(1, NY)]
    for copy in copies:
        copy.wait_recv()

    for b in range(5):
        low = (y - b + 4) // 4
        layer = 1 - low
        i = low * y + (1 - low) * (3 - y)
        j = low * b + (1 - low) * (b - y - 1)
        left = panel_ref[layer, :, span(i * B, B)]
        right = panel_ref[layer, :, span(j * B, B)]
        mine[b * B : b * B + B, :] = lax.dot_general(left, right, TN, preferred_element_type=F32)

    copy = go(mine.at[span((1 - c) * 320, 320), :], core_buf, along("c", spot, 1))
    copy.wait_recv()
    chip[...] = mine[span(c * 320, 320), :] + core_buf[...]
    copies = [
        go(chip.at[span(((z + k) % NZ) * 40, 40), :], z_buf.at[k - 1], along("z", spot, k)) for k in range(1, NZ)
    ]
    total = chip[span(z * 40, 40), :]
    for k, copy in enumerate(copies):
        copy.wait_recv()
        total = total + z_buf[k]
    strip[...] = total
    copies = [go(strip, x_buf.at[k - 1], along("x", spot, k)) for k in range(1, NX)]
    for k, copy in enumerate(copies):
        copy.wait_recv()
        total = total + x_buf[k]
    place_of = pl.ds(pl.multiple_of(c * 320 + z * 40, 8), 40)
    blocks_ref[y, place_of, :] = total
    piece = blocks_ref.at[y, place_of, :]
    copies = [go(piece, piece, along("z", spot, k)) for k in range(1, NZ)]
    for copy in copies:
        copy.wait_recv()
    piece = blocks_ref.at[y, span(c * 320, 320), :]
    copies = [go(piece, piece, along("y", spot, k)) for k in range(1, NY)]
    for copy in copies:
        copy.wait_recv()
    piece = blocks_ref.at[:, span(c * 320, 320), :]
    go(piece, piece, along("c", spot, 1)).wait_recv()
    for copy in done:
        copy.wait_send()


def gram(part):
    vmem = pl.BlockSpec(memory_space=pltpu.VMEM)
    return pl.pallas_call(
        gram_kernel,
        out_shape=(
            jax.ShapeDtypeStruct((LAYERS, ROWS, RANK), BF),
            jax.ShapeDtypeStruct((4, 640, B), F32),
        ),
        in_specs=[vmem],
        out_specs=(vmem, vmem),
        scratch_shapes=[
            pltpu.VMEM((NY - 1, LAYERS, ROWS // NY, RANK), BF),
            pltpu.VMEM((640, B), F32),
            pltpu.VMEM((320, B), F32),
            pltpu.VMEM((320, B), F32),
            pltpu.VMEM((NZ - 1, 40, B), F32),
            pltpu.VMEM((40, B), F32),
            pltpu.VMEM((NX - 1, 40, B), F32),
            pltpu.SemaphoreType.DMA((2, 32)),
        ],
        compiler_params=pltpu.CompilerParams(collective_id=0, has_side_effects=True, vmem_limit_bytes=32 << 20),
    )(part)


def eliminate(tiles):
    lane = lax.broadcasted_iota(jnp.int32, (8, B), 1)
    sub = lax.broadcasted_iota(jnp.int32, (8, B), 0)
    for j in range(B):
        first, at = divmod(j, 8)
        for rows in tiles:
            row = rows[first][at : at + 1, :]
            inverse = 1.0 / row[:, j : j + 1]
            scaled = jnp.where(lane == j, 1.0, jnp.broadcast_to(row, (8, B))) * inverse
            for t in range(first, B // 8):
                if t == first and at == 7:
                    continue
                column = jnp.broadcast_to(rows[t][:, j : j + 1], (8, B))
                new = jnp.where(lane == j, 0.0, rows[t]) - column * scaled
                rows[t] = jnp.where(sub > at, new, rows[t]) if t == first else new
    return tiles


def finish(rows):
    whole = jnp.concatenate(rows, axis=0)
    r = lax.broadcasted_iota(jnp.int32, (B, B), 0)
    q = lax.broadcasted_iota(jnp.int32, (B, B), 1)
    pivot = jnp.sum(jnp.where(r == q, whole, 0.0), axis=1, keepdims=True)
    return jnp.where(q < r, whole, jnp.where(q == r, 1.0, 0.0)) * lax.rsqrt(pivot)


def factor_kernel(blocks_ref, panel_ref, basis_ref, w):
    for i in range(4):
        for j in range(i + 1):
            for layer, (who, at) in enumerate(((i, j), (3 - i, 4 - i + j))):
                block = blocks_ref[who, at * B : at * B + B, :]
                w[layer, i * B : i * B + B, j * B : j * B + B] = block
                if i != j:
                    w[layer, j * B : j * B + B, i * B : i * B + B] = block.T

    def step(k, carry):
        here = span(k * B, B)
        tiles = [[w[n, span(k * B + 8 * t, 8), here] for t in range(B // 8)] for n in range(LAYERS)]
        tiles = eliminate(tiles)
        r = lax.broadcasted_iota(jnp.int32, (RANK, 1), 0)
        q = lax.broadcasted_iota(jnp.int32, (1, RANK), 1)
        eye = lax.broadcasted_iota(jnp.int32, (B, RANK), 0) + k * B == lax.broadcasted_iota(jnp.int32, (B, RANK), 1)
        inside = (q >= k * B) & (q < k * B + B)
        below = r >= k * B + B
        for n in range(LAYERS):
            inverse = finish(tiles[n])
            top = jnp.where(inside, eye.astype(F32), w[n, here, :])
            right = jnp.dot(inverse, top, precision=HIGHEST, preferred_element_type=F32)
            left = lax.dot_general(w[n, :, here], inverse, NT, precision=HIGHEST, preferred_element_type=F32)
            left = jnp.where(below, left, 0.0)
            rest = jnp.where(inside & below, 0.0, w[n])
            w[n] = rest - jnp.dot(left, right, precision=HIGHEST, preferred_element_type=F32)
            w[n, here, :] = jnp.where(q < k * B + B, right, 0.0)
        return carry

    lax.fori_loop(0, 4, step, 0)
    for n in range(LAYERS):
        basis = lax.dot_general(panel_ref[n].astype(F32), w[n], NT, precision=HIGHEST, preferred_element_type=F32)
        basis_ref[n] = basis.astype(BF)


def factor(blocks, panel):
    vmem = pl.BlockSpec(memory_space=pltpu.VMEM)
    return pl.pallas_call(
        factor_kernel,
        out_shape=jax.ShapeDtypeStruct((LAYERS, ROWS, RANK), BF),
        in_specs=[vmem, vmem],
        out_specs=vmem,
        scratch_shapes=[pltpu.VMEM((LAYERS, RANK, RANK), F32)],
        compiler_params=pltpu.CompilerParams(vmem_limit_bytes=32 << 20),
    )(blocks, panel)


def tail_kernel(
    basis_ref,
    summed_ref,
    first_ref,
    second_ref,
    new_first_ref,
    new_second_ref,
    delta_ref,
    twin_basis,
    twin_summed,
    x_out,
    x_in,
    x_own,
    z_out,
    z_in,
    z_own,
    full,
    fresh,
    joined,
    gathered,
    sems,
):
    spot = place()
    y, x, z, c = spot
    peers = [along("c", spot, 1)]
    peers += [along("x", spot, k) for k in range(1, NX)]
    peers += [along("z", spot, k) for k in range(1, NZ)]
    greet(peers)
    done = []
    count = [0]

    def go(src, dst, peer):
        copy = ship(src, dst, sems.at[0, count[0]], sems.at[1, count[0]], peer)
        count[0] += 1
        done.append(copy)
        return copy

    mine, other = span(c * HALF, HALF), span((1 - c) * HALF, HALF)
    twin = along("c", spot, 1)
    got = [
        (go(basis_ref.at[n], twin_basis.at[n], twin), go(summed_ref.at[n, :, other], twin_summed.at[n], twin))
        for n in range(LAYERS)
    ]

    def product(n, part):
        here = span(part * B, B)
        out = lax.dot_general(basis_ref[n, :, here], summed_ref[n, :, mine], TN, preferred_element_type=F32)
        return out + lax.dot_general(twin_basis[n, :, here], twin_summed[n], TN, preferred_element_type=F32)

    x_copies = []
    for n in range(LAYERS):
        for copy in got[n]:
            copy.wait_recv()
        copies = []
        for k in (2, 1, 3):
            x_out[n, k - 1] = product(n, (x + k) % NX).astype(BF)
            copies.append((k, go(x_out.at[n, k - 1], x_in.at[n, k - 1], along("x", spot, k))))
        x_own[n] = product(n, x)
        x_copies.append(copies)

    z_copies = []
    for n in range(LAYERS):
        for k, copy in x_copies[n]:
            copy.wait_recv()
        total = x_own[n]
        for k in range(1, NX):
            total = total + x_in[n, k - 1].astype(F32)
        x_own[n] = total
        z_out[n] = total.astype(BF)
        z_own[n] = x_own[n, span(z * 16, 16), :]
        z_copies.append(
            [go(z_out.at[n, span(((z + k) % NZ) * 16, 16), :], z_in.at[n, k - 1], along("z", spot, k)) for k in range(1, NZ)]
        )
    for n in range(LAYERS):
        total = z_own[n]
        for k, copy in enumerate(z_copies[n]):
            copy.wait_recv()
            total = total + z_in[n, k].astype(F32)
        z_own[n] = total

    copy = go(z_own.at[:, span((1 - c) * 8, 8), :], full.at[:, :, mine], twin)
    full[:, :, mine] = z_own[:, span(c * 8, 8), :]
    copy.wait_recv()
    for n in range(LAYERS):
        projected = full[n]
        new_first = 0.9 * first_ref[:, n, :] + 0.1 * projected
        new_second = 0.999 * second_ref[:, n, :] + 0.001 * projected * projected
        new_first_ref[:, n, :] = new_first
        new_second_ref[:, n, :] = new_second
        fresh[n] = new_first / (jnp.sqrt(new_second) + 1e-08)
    rows = span(c * 8, 8)
    copy = go(fresh.at[:, :, other], joined.at[:, rows, :], twin)
    joined[:, rows, :] = fresh[:, :, mine]
    copy.wait_recv()

    slot = span(x * B + z * 16, 16)
    gathered[c, :, slot, :] = joined[...].astype(BF)
    piece = gathered.at[c, :, slot, :]
    copies = [go(piece, piece, along("z", spot, k)) for k in range(1, NZ)]
    for copy in copies:
        copy.wait_recv()
    piece = gathered.at[c, :, span(x * B, B), :]
    copies = [(k, go(piece, piece, along("x", spot, k))) for k in (2, 1, 3)]
    crossed = [go(piece, piece, twin)]
    for k, copy in copies[1:] + copies[:1]:
        copy.wait_recv()
        piece = gathered.at[c, :, span(((x - k + NX) % NX) * B, B), :]
        crossed.append(go(piece, piece, twin))
    for copy in crossed:
        copy.wait_recv()

    tile = 256
    for n in range(LAYERS):
        for half in range(2):

            def body(t, carry):
                right = gathered[half, n, :, span(t * tile, tile)]
                out = jnp.dot(basis_ref[n], right, preferred_element_type=F32)
                delta_ref[n, :, span(half * HALF + t * tile, tile)] = out.astype(BF)
                return carry

            lax.fori_loop(0, HALF // tile, body, 0)
    for copy in done:
        copy.wait_send()


def tail(basis, summed, first, second):
    vmem = pl.BlockSpec(memory_space=pltpu.VMEM)
    return pl.pallas_call(
        tail_kernel,
        out_shape=(
            jax.ShapeDtypeStruct((8, LAYERS, OWN), F32),
            jax.ShapeDtypeStruct((8, LAYERS, OWN), F32),
            jax.ShapeDtypeStruct((LAYERS, ROWS, OWN), BF),
        ),
        in_specs=[vmem] * 4,
        out_specs=(vmem,) * 3,
        scratch_shapes=[
            pltpu.VMEM((LAYERS, ROWS, RANK), BF),
            pltpu.VMEM((LAYERS, ROWS, HALF), BF),
            pltpu.VMEM((LAYERS, NX - 1, B, HALF), BF),
            pltpu.VMEM((LAYERS, NX - 1, B, HALF), BF),
            pltpu.VMEM((LAYERS, B, HALF), F32),
            pltpu.VMEM((LAYERS, B, HALF), BF),
            pltpu.VMEM((LAYERS, NZ - 1, 16, HALF), BF),
            pltpu.VMEM((LAYERS, 16, HALF), F32),
            pltpu.VMEM((LAYERS, 8, OWN), F32),
            pltpu.VMEM((LAYERS, 8, OWN), F32),
            pltpu.VMEM((LAYERS, 16, HALF), F32),
            pltpu.VMEM((2, LAYERS, RANK, HALF), BF),
            pltpu.SemaphoreType.DMA((2, 48)),
        ],
        compiler_params=pltpu.CompilerParams(collective_id=1, has_side_effects=True, vmem_limit_bytes=48 << 20),
    )(basis, summed, first, second)


def local(grad_parts, omega, first_moment, second_moment):
    summed = lax.psum_scatter(grad_parts[0], "dp", scatter_dimension=2, tiled=True)
    part = jnp.einsum("lrd,dk->lrk", summed, omega, preferred_element_type=F32).astype(BF)
    panel, blocks = gram(part)
    basis = factor(blocks, panel)
    return tail(basis, summed, first_moment, second_moment)


def solution(mesh):
    return jax.shard_map(
        local,
        mesh=mesh,
        in_specs=(P("dp", None, "mp", None), P("dp", None), P("mp", None, "dp"), P("mp", None, "dp")),
        out_specs=(P("mp", None, "dp"), P("mp", None, "dp"), P(None, "mp", "dp")),
        check_vma=False,
    )
```

```python
import functools

import jax
import jax.numpy as jnp
from jax import lax
from jax.experimental import pallas as pl
from jax.experimental.pallas import tpu as pltpu
from jax.sharding import PartitionSpec as P

HIGHEST = lax.Precision.HIGHEST
MESH = pl.DeviceIdType.MESH
NT = (((1,), (1,)), ((), ()))
TN = (((0,), (0,)), ((), ()))
BF = jnp.bfloat16
F32 = jnp.float32

LAYERS = 2
ROWS = 256
D = 8192
OWN = 2048
HALF = 1024
RANK = 512
B = 128
NY, NX, NZ, NC = 4, 4, 8, 2


def place():
    mp = lax.axis_index("mp")
    return lax.axis_index("dp"), mp // (NZ * NC), (mp // NC) % NZ, mp % NC


def device(y, x, z, c):
    return {"dp": y, "mp": x * (NZ * NC) + z * NC + c}


def greet(peers):
    barrier = pltpu.get_barrier_semaphore()
    for peer in peers:
        pl.semaphore_signal(barrier, inc=1, device_id=peer, device_id_type=MESH)
    pl.semaphore_wait(barrier, len(peers))


def along(axis, spot, k):
    y, x, z, c = spot
    if axis == "y":
        return device((y + k) % NY, x, z, c)
    if axis == "x":
        return device(y, (x + k) % NX, z, c)
    if axis == "z":
        return device(y, x, (z + k) % NZ, c)
    return device(y, x, z, 1 - c)


def ship(src, dst, send, recv, peer):
    copy = pltpu.make_async_remote_copy(
        src_ref=src, dst_ref=dst, send_sem=send, recv_sem=recv, device_id=peer, device_id_type=MESH
    )
    copy.start()
    return copy


def span(start, size):
    return pl.ds(pl.multiple_of(start, size), size)


def panel_kernel(omega_ref, grads_hbm, part_ref, grads, far, total, sems, local_sems):
    spot = place()
    y, x, z, c = spot
    up, down, twin = along("y", spot, 1), along("y", spot, NY - 1), along("c", spot, 1)
    order = (0, NY - 1, 1, 2)
    loads = []
    for k in order:
        columns = span(((y + k) % NY) * OWN, OWN)
        load = pltpu.make_async_copy(grads_hbm.at[:, :, columns], grads.at[k], local_sems.at[k])
        load.start()
        loads.append(load)
    greet([up, down, twin])
    done = []
    count = [0]

    def go(src, dst, peer):
        copy = ship(src, dst, sems.at[0, count[0]], sems.at[1, count[0]], peer)
        count[0] += 1
        done.append(copy)
        return copy

    q = OWN // 4
    rows = [span(c * 2 * q + h * q, q) for h in range(2)]
    near = [None] * 4
    near[0] = go(omega_ref.at[rows[0], :], far.at[0, rows[0], :], up)
    near[1] = go(omega_ref.at[rows[1], :], far.at[1, rows[1], :], down)
    near[2] = go(omega_ref.at[rows[1], :], far.at[0, rows[1], :], up)
    near[3] = go(omega_ref.at[rows[0], :], far.at[1, rows[0], :], down)

    def add(k, matrix, fresh):
        for n in range(LAYERS):
            out = jnp.dot(grads[k, n], matrix[...], preferred_element_type=F32)
            total[n] = out if fresh else total[n] + out

    loads[0].wait()
    add(0, omega_ref, True)
    near[0].wait_recv()
    relay = [go(far.at[0, rows[0], :], far.at[2, rows[0], :], up)]
    crossed = [go(far.at[0, rows[0], :], far.at[0, rows[0], :], twin)]
    near[1].wait_recv()
    relay.append(go(far.at[1, rows[1], :], far.at[2, rows[1], :], down))
    crossed.append(go(far.at[1, rows[1], :], far.at[1, rows[1], :], twin))
    near[2].wait_recv()
    crossed.append(go(far.at[0, rows[1], :], far.at[0, rows[1], :], twin))
    near[3].wait_recv()
    crossed.append(go(far.at[1, rows[0], :], far.at[1, rows[0], :], twin))
    crossed[0].wait_recv()
    crossed[2].wait_recv()
    loads[1].wait()
    add(NY - 1, far.at[0], False)
    crossed[1].wait_recv()
    crossed[3].wait_recv()
    loads[2].wait()
    add(1, far.at[1], False)
    for h, copy in enumerate(relay):
        copy.wait_recv()
        crossed.append(go(far.at[2, rows[h], :], far.at[2, rows[h], :], twin))
    crossed[4].wait_recv()
    crossed[5].wait_recv()
    loads[3].wait()
    add(2, far.at[2], False)
    part_ref[...] = total[...].astype(BF)
    for copy in done:
        copy.wait_send()


def panel_part(omega, grads):
    vmem = pl.BlockSpec(memory_space=pltpu.VMEM)
    return pl.pallas_call(
        panel_kernel,
        out_shape=jax.ShapeDtypeStruct((LAYERS, ROWS, RANK), BF),
        in_specs=[vmem, pl.BlockSpec(memory_space=pl.ANY)],
        out_specs=vmem,
        scratch_shapes=[
            pltpu.VMEM((NY, LAYERS, ROWS, OWN), BF),
            pltpu.VMEM((NY - 1, OWN, RANK), BF),
            pltpu.VMEM((LAYERS, ROWS, RANK), F32),
            pltpu.SemaphoreType.DMA((2, 12)),
            pltpu.SemaphoreType.DMA((NY,)),
        ],
        compiler_params=pltpu.CompilerParams(collective_id=2, has_side_effects=True, vmem_limit_bytes=48 << 20),
    )(omega, grads)


def gram_kernel(part_ref, panel_ref, blocks_ref, rs_buf, mine, core_buf, chip, z_buf, strip, x_buf, sems):
    spot = place()
    y, x, z, c = spot
    peers = [along("y", spot, k) for k in range(1, NY)]
    peers += [along("z", spot, k) for k in range(1, NZ)]
    peers += [along("x", spot, k) for k in range(1, NX)]
    peers += [along("c", spot, 1)]
    greet(peers)
    done = []
    count = [0]

    def go(src, dst, peer):
        copy = ship(src, dst, sems.at[0, count[0]], sems.at[1, count[0]], peer)
        count[0] += 1
        done.append(copy)
        return copy

    q = ROWS // NY
    own = span(y * q, q)
    copies = [
        go(part_ref.at[:, span(((y + k) % NY) * q, q), :], rs_buf.at[k - 1], along("y", spot, k)) for k in range(1, NY)
    ]
    total = part_ref[:, own, :].astype(F32)
    for k, copy in enumerate(copies):
        copy.wait_recv()
        total = total + rs_buf[k].astype(F32)
    panel_ref[:, own, :] = total.astype(BF)
    copies = [go(panel_ref.at[:, own, :], panel_ref.at[:, own, :], along("y", spot, k)) for k in range(1, NY)]
    for copy in copies:
        copy.wait_recv()

    for b in range(5):
        low = (y - b + 4) // 4
        layer = 1 - low
        i = low * y + (1 - low) * (3 - y)
        j = low * b + (1 - low) * (b - y - 1)
        left = panel_ref[layer, :, span(i * B, B)]
        right = panel_ref[layer, :, span(j * B, B)]
        mine[b * B : b * B + B, :] = lax.dot_general(left, right, TN, preferred_element_type=F32)

    copy = go(mine.at[span((1 - c) * 320, 320), :], core_buf, along("c", spot, 1))
    copy.wait_recv()
    chip[...] = mine[span(c * 320, 320), :] + core_buf[...]
    copies = [
        go(chip.at[span(((z + k) % NZ) * 40, 40), :], z_buf.at[k - 1], along("z", spot, k)) for k in range(1, NZ)
    ]
    total = chip[span(z * 40, 40), :]
    for k, copy in enumerate(copies):
        copy.wait_recv()
        total = total + z_buf[k]
    strip[...] = total
    copies = [go(strip, x_buf.at[k - 1], along("x", spot, k)) for k in range(1, NX)]
    for k, copy in enumerate(copies):
        copy.wait_recv()
        total = total + x_buf[k]
    place_of = pl.ds(pl.multiple_of(c * 320 + z * 40, 8), 40)
    blocks_ref[y, place_of, :] = total
    piece = blocks_ref.at[y, place_of, :]
    copies = [go(piece, piece, along("z", spot, k)) for k in range(1, NZ)]
    for copy in copies:
        copy.wait_recv()
    piece = blocks_ref.at[y, span(c * 320, 320), :]
    copies = [go(piece, piece, along("y", spot, k)) for k in range(1, NY)]
    for copy in copies:
        copy.wait_recv()
    piece = blocks_ref.at[:, span(c * 320, 320), :]
    go(piece, piece, along("c", spot, 1)).wait_recv()
    for copy in done:
        copy.wait_send()


def gram(part):
    vmem = pl.BlockSpec(memory_space=pltpu.VMEM)
    return pl.pallas_call(
        gram_kernel,
        out_shape=(
            jax.ShapeDtypeStruct((LAYERS, ROWS, RANK), BF),
            jax.ShapeDtypeStruct((4, 640, B), F32),
        ),
        in_specs=[vmem],
        out_specs=(vmem, vmem),
        scratch_shapes=[
            pltpu.VMEM((NY - 1, LAYERS, ROWS // NY, RANK), BF),
            pltpu.VMEM((640, B), F32),
            pltpu.VMEM((320, B), F32),
            pltpu.VMEM((320, B), F32),
            pltpu.VMEM((NZ - 1, 40, B), F32),
            pltpu.VMEM((40, B), F32),
            pltpu.VMEM((NX - 1, 40, B), F32),
            pltpu.SemaphoreType.DMA((2, 32)),
        ],
        compiler_params=pltpu.CompilerParams(collective_id=0, has_side_effects=True, vmem_limit_bytes=32 << 20),
    )(part)


def eliminate(tiles):
    lane = lax.broadcasted_iota(jnp.int32, (8, B), 1)
    sub = lax.broadcasted_iota(jnp.int32, (8, B), 0)
    count = B // 8

    def spread(tile, k):
        return jnp.broadcast_to(tile[k : k + 1, :], (8, B))

    def columns(tile, b):
        return [jnp.broadcast_to(tile[:, 8 * b + k : 8 * b + k + 1], (8, B)) for k in range(8)]

    found = [[None] * count for _ in tiles]
    for b in range(count):
        inside = (lane >= 8 * b) & (lane < 8 * b + 8)
        unit = (lane == sub + 8 * b).astype(F32)
        states = []
        for rows in tiles:
            start = jnp.where(inside, unit, rows[b])
            states.append([columns(rows[b], b), start, start, jnp.zeros((8, B), F32)])
        for k in range(8):
            for state in states:
                cols, jordan, forward, scale = state
                pivot = spread(cols[k], k)
                inverse = 1.0 / pivot
                factor = cols[k] * inverse
                for j in range(k + 1, 8):
                    line = spread(cols[j], k)
                    cols[j] = jnp.where(sub == k, line * inverse, cols[j] - factor * line)
                line = spread(jordan, k)
                state[1] = jnp.where(sub == k, line * inverse, jordan - factor * line)
                state[2] = jnp.where(sub > k, forward - factor * spread(forward, k), forward)
                state[3] = jnp.where(sub == k, pivot, scale)
        for n, rows in enumerate(tiles):
            cols, jordan, forward, scale = states[n]
            found[n][b] = jnp.where(lane < 8 * b + 8, forward, 0.0) * lax.rsqrt(scale)
            lines = [spread(jordan, k) for k in range(8)]
            for t in range(b + 1, count):
                cols = columns(rows[t], b)
                terms = [cols[k] * lines[k] for k in range(8)]
                while len(terms) > 1:
                    terms = [terms[i] + terms[i + 1] for i in range(0, len(terms), 2)]
                rows[t] = jnp.where(inside, 0.0, rows[t]) - terms[0]
    return found


def finish(rows):
    return jnp.concatenate(rows, axis=0)


def factor_kernel(blocks_ref, panel_ref, basis_ref, w, inv):
    for i in range(4):
        for j in range(i + 1):
            for layer, (who, at) in enumerate(((i, j), (3 - i, 4 - i + j))):
                block = blocks_ref[who, at * B : at * B + B, :]
                w[layer, i * B : i * B + B, j * B : j * B + B] = block
                if i != j:
                    w[layer, j * B : j * B + B, i * B : i * B + B] = block.T

    def step(k, carry):
        here = span(k * B, B)
        tiles = [[w[n, span(k * B + 8 * t, 8), here] for t in range(B // 8)] for n in range(LAYERS)]
        tiles = eliminate(tiles)
        r = lax.broadcasted_iota(jnp.int32, (RANK, 1), 0)
        q = lax.broadcasted_iota(jnp.int32, (1, RANK), 1)
        eye = lax.broadcasted_iota(jnp.int32, (B, RANK), 0) + k * B == lax.broadcasted_iota(jnp.int32, (B, RANK), 1)
        inside = (q >= k * B) & (q < k * B + B)
        below = r >= k * B + B
        for n in range(LAYERS):
            inv[n] = finish(tiles[n])
        for at in range(4):

            @pl.when(k == at)
            def _():
                a, z = at * B, at * B + B
                for n in range(LAYERS):
                    inverse = inv[n]
                    right = jnp.dot(inverse, w[n, a:z, :], precision=HIGHEST, preferred_element_type=F32)
                    pieces = [right[:, :a], inverse, right[:, z:]]
                    right = jnp.concatenate([p for p in pieces if p.shape[1]], axis=1)
                    if z < RANK:
                        left = lax.dot_general(
                            w[n, z:, a:z], inverse, NT, precision=HIGHEST, preferred_element_type=F32
                        )
                        w[n, z:, a:z] = jnp.zeros((RANK - z, B), F32)
                        w[n, z:, :] = w[n, z:, :] - jnp.dot(
                            left, right, precision=HIGHEST, preferred_element_type=F32
                        )
                        right = jnp.concatenate([right[:, :z], jnp.zeros((B, RANK - z), F32)], axis=1)
                    w[n, a:z, :] = right

        return carry

    lax.fori_loop(0, 4, step, 0)
    for n in range(LAYERS):
        rest = w[n]
        basis = jnp.zeros((ROWS, RANK), F32)
        for _ in range(3):
            part = rest.astype(BF)
            rest = rest - part.astype(F32)
            basis = basis + lax.dot_general(panel_ref[n], part, NT, preferred_element_type=F32)
        basis_ref[n] = basis.astype(BF)


def factor(blocks, panel):
    vmem = pl.BlockSpec(memory_space=pltpu.VMEM)
    return pl.pallas_call(
        factor_kernel,
        out_shape=jax.ShapeDtypeStruct((LAYERS, ROWS, RANK), BF),
        in_specs=[vmem, vmem],
        out_specs=vmem,
        scratch_shapes=[pltpu.VMEM((LAYERS, RANK, RANK), F32), pltpu.VMEM((LAYERS, B, B), F32)],
        compiler_params=pltpu.CompilerParams(vmem_limit_bytes=32 << 20),
    )(blocks, panel)


def tail_kernel(
    basis_ref,
    summed_ref,
    first_ref,
    second_ref,
    new_first_ref,
    new_second_ref,
    delta_ref,
    twin_basis,
    twin_summed,
    x_out,
    x_in,
    x_own,
    z_out,
    z_in,
    z_own,
    full,
    fresh,
    joined,
    gathered,
    sems,
):
    spot = place()
    y, x, z, c = spot
    peers = [along("c", spot, 1)]
    peers += [along("x", spot, k) for k in range(1, NX)]
    peers += [along("z", spot, k) for k in range(1, NZ)]
    greet(peers)
    done = []
    count = [0]

    def go(src, dst, peer):
        copy = ship(src, dst, sems.at[0, count[0]], sems.at[1, count[0]], peer)
        count[0] += 1
        done.append(copy)
        return copy

    mine, other = span(c * HALF, HALF), span((1 - c) * HALF, HALF)
    twin = along("c", spot, 1)
    got = [
        (go(basis_ref.at[n], twin_basis.at[n], twin), go(summed_ref.at[n, :, other], twin_summed.at[n], twin))
        for n in range(LAYERS)
    ]

    def product(n, part):
        here = span(part * B, B)
        out = lax.dot_general(basis_ref[n, :, here], summed_ref[n, :, mine], TN, preferred_element_type=F32)
        return out + lax.dot_general(twin_basis[n, :, here], twin_summed[n], TN, preferred_element_type=F32)

    x_copies = []
    for n in range(LAYERS):
        for copy in got[n]:
            copy.wait_recv()
        copies = []
        for k in (2, 1, 3):
            x_out[n, k - 1] = product(n, (x + k) % NX).astype(BF)
            copies.append((k, go(x_out.at[n, k - 1], x_in.at[n, k - 1], along("x", spot, k))))
        x_own[n] = product(n, x)
        x_copies.append(copies)

    z_copies = []
    for n in range(LAYERS):
        for k, copy in x_copies[n]:
            copy.wait_recv()
        total = x_own[n]
        for k in range(1, NX):
            total = total + x_in[n, k - 1].astype(F32)
        x_own[n] = total
        z_out[n] = total.astype(BF)
        z_own[n] = x_own[n, span(z * 16, 16), :]
        z_copies.append(
            [go(z_out.at[n, span(((z + k) % NZ) * 16, 16), :], z_in.at[n, k - 1], along("z", spot, k)) for k in range(1, NZ)]
        )
    for n in range(LAYERS):
        total = z_own[n]
        for k, copy in enumerate(z_copies[n]):
            copy.wait_recv()
            total = total + z_in[n, k].astype(F32)
        z_own[n] = total

    copy = go(z_own.at[:, span((1 - c) * 8, 8), :], full.at[:, :, mine], twin)
    full[:, :, mine] = z_own[:, span(c * 8, 8), :]
    copy.wait_recv()
    for n in range(LAYERS):
        projected = full[n]
        new_first = 0.9 * first_ref[:, n, :] + 0.1 * projected
        new_second = 0.999 * second_ref[:, n, :] + 0.001 * projected * projected
        new_first_ref[:, n, :] = new_first
        new_second_ref[:, n, :] = new_second
        fresh[n] = new_first / (jnp.sqrt(new_second) + 1e-08)
    rows = span(c * 8, 8)
    copy = go(fresh.at[:, :, other], joined.at[:, rows, :], twin)
    joined[:, rows, :] = fresh[:, :, mine]
    copy.wait_recv()

    slot = span(x * B + z * 16, 16)
    gathered[c, :, slot, :] = joined[...].astype(BF)
    piece = gathered.at[c, :, slot, :]
    copies = [go(piece, piece, along("z", spot, k)) for k in range(1, NZ)]
    for copy in copies:
        copy.wait_recv()
    piece = gathered.at[c, :, span(x * B, B), :]
    copies = [(k, go(piece, piece, along("x", spot, k))) for k in (2, 1, 3)]
    crossed = [go(piece, piece, twin)]
    for k, copy in copies[1:] + copies[:1]:
        copy.wait_recv()
        piece = gathered.at[c, :, span(((x - k + NX) % NX) * B, B), :]
        crossed.append(go(piece, piece, twin))
    for copy in crossed:
        copy.wait_recv()

    tile = 256
    for n in range(LAYERS):
        for half in range(2):

            def body(t, carry):
                right = gathered[half, n, :, span(t * tile, tile)]
                out = jnp.dot(basis_ref[n], right, preferred_element_type=F32)
                delta_ref[n, :, span(half * HALF + t * tile, tile)] = out.astype(BF)
                return carry

            lax.fori_loop(0, HALF // tile, body, 0)
    for copy in done:
        copy.wait_send()


def tail(basis, summed, first, second):
    vmem = pl.BlockSpec(memory_space=pltpu.VMEM)
    return pl.pallas_call(
        tail_kernel,
        out_shape=(
            jax.ShapeDtypeStruct((8, LAYERS, OWN), F32),
            jax.ShapeDtypeStruct((8, LAYERS, OWN), F32),
            jax.ShapeDtypeStruct((LAYERS, ROWS, OWN), BF),
        ),
        in_specs=[vmem] * 4,
        out_specs=(vmem,) * 3,
        scratch_shapes=[
            pltpu.VMEM((LAYERS, ROWS, RANK), BF),
            pltpu.VMEM((LAYERS, ROWS, HALF), BF),
            pltpu.VMEM((LAYERS, NX - 1, B, HALF), BF),
            pltpu.VMEM((LAYERS, NX - 1, B, HALF), BF),
            pltpu.VMEM((LAYERS, B, HALF), F32),
            pltpu.VMEM((LAYERS, B, HALF), BF),
            pltpu.VMEM((LAYERS, NZ - 1, 16, HALF), BF),
            pltpu.VMEM((LAYERS, 16, HALF), F32),
            pltpu.VMEM((LAYERS, 8, OWN), F32),
            pltpu.VMEM((LAYERS, 8, OWN), F32),
            pltpu.VMEM((LAYERS, 16, HALF), F32),
            pltpu.VMEM((2, LAYERS, RANK, HALF), BF),
            pltpu.SemaphoreType.DMA((2, 48)),
        ],
        compiler_params=pltpu.CompilerParams(collective_id=1, has_side_effects=True, vmem_limit_bytes=48 << 20),
    )(basis, summed, first, second)


def local(grad_parts, omega, first_moment, second_moment):
    part = panel_part(omega, grad_parts[0])
    grads, part = lax.optimization_barrier((grad_parts[0], part))
    summed = lax.psum_scatter(grads, "dp", scatter_dimension=2, tiled=True)
    panel, blocks = gram(part)
    basis = factor(blocks, panel)
    return tail(basis, summed, first_moment, second_moment)


def solution(mesh):
    return jax.shard_map(
        local,
        mesh=mesh,
        in_specs=(P("dp", None, "mp", None), P("dp", None), P("mp", None, "dp"), P("mp", None, "dp")),
        out_specs=(P("mp", None, "dp"), P("mp", None, "dp"), P(None, "mp", "dp")),
        check_vma=False,
    )
```

```python
import functools

import jax
import jax.numpy as jnp
from jax import lax
from jax.experimental import pallas as pl
from jax.experimental.pallas import tpu as pltpu
from jax.sharding import PartitionSpec as P

HIGHEST = lax.Precision.HIGHEST
MESH = pl.DeviceIdType.MESH
NT = (((1,), (1,)), ((), ()))
TN = (((0,), (0,)), ((), ()))
BF = jnp.bfloat16
F32 = jnp.float32

LAYERS = 2
ROWS = 256
D = 8192
OWN = 2048
HALF = 1024
RANK = 512
B = 128
NY, NX, NZ, NC = 4, 4, 8, 2


def place():
    mp = lax.axis_index("mp")
    return lax.axis_index("dp"), mp // (NZ * NC), (mp // NC) % NZ, mp % NC


def device(y, x, z, c):
    return {"dp": y, "mp": x * (NZ * NC) + z * NC + c}


def greet(peers):
    barrier = pltpu.get_barrier_semaphore()
    for peer in peers:
        pl.semaphore_signal(barrier, inc=1, device_id=peer, device_id_type=MESH)
    pl.semaphore_wait(barrier, len(peers))


def along(axis, spot, k):
    y, x, z, c = spot
    if axis == "y":
        return device((y + k) % NY, x, z, c)
    if axis == "x":
        return device(y, (x + k) % NX, z, c)
    if axis == "z":
        return device(y, x, (z + k) % NZ, c)
    return device(y, x, z, 1 - c)


def ship(src, dst, send, recv, peer):
    copy = pltpu.make_async_remote_copy(
        src_ref=src, dst_ref=dst, send_sem=send, recv_sem=recv, device_id=peer, device_id_type=MESH
    )
    copy.start()
    return copy


def span(start, size):
    return pl.ds(pl.multiple_of(start, size), size)


def panel_kernel(omega_ref, grads_hbm, part_ref, grads, far, total, sems, local_sems):
    spot = place()
    y, x, z, c = spot
    up, down, twin = along("y", spot, 1), along("y", spot, NY - 1), along("c", spot, 1)
    order = (0, NY - 1, 1, 2)
    loads = []
    for k in order:
        columns = span(((y + k) % NY) * OWN, OWN)
        load = pltpu.make_async_copy(grads_hbm.at[:, :, columns], grads.at[k], local_sems.at[k])
        load.start()
        loads.append(load)
    greet([up, down, twin])
    done = []
    count = [0]

    def go(src, dst, peer):
        copy = ship(src, dst, sems.at[0, count[0]], sems.at[1, count[0]], peer)
        count[0] += 1
        done.append(copy)
        return copy

    q = OWN // 4
    rows = [span(c * 2 * q + h * q, q) for h in range(2)]
    near = [None] * 4
    near[0] = go(omega_ref.at[rows[0], :], far.at[0, rows[0], :], up)
    near[1] = go(omega_ref.at[rows[1], :], far.at[1, rows[1], :], down)
    near[2] = go(omega_ref.at[rows[1], :], far.at[0, rows[1], :], up)
    near[3] = go(omega_ref.at[rows[0], :], far.at[1, rows[0], :], down)

    def add(k, matrix, fresh):
        for n in range(LAYERS):
            out = jnp.dot(grads[k, n], matrix[...], preferred_element_type=F32)
            total[n] = out if fresh else total[n] + out

    loads[0].wait()
    add(0, omega_ref, True)
    near[0].wait_recv()
    relay = [go(far.at[0, rows[0], :], far.at[2, rows[0], :], up)]
    crossed = [go(far.at[0, rows[0], :], far.at[0, rows[0], :], twin)]
    near[1].wait_recv()
    relay.append(go(far.at[1, rows[1], :], far.at[2, rows[1], :], down))
    crossed.append(go(far.at[1, rows[1], :], far.at[1, rows[1], :], twin))
    near[2].wait_recv()
    crossed.append(go(far.at[0, rows[1], :], far.at[0, rows[1], :], twin))
    near[3].wait_recv()
    crossed.append(go(far.at[1, rows[0], :], far.at[1, rows[0], :], twin))
    crossed[0].wait_recv()
    crossed[2].wait_recv()
    loads[1].wait()
    add(NY - 1, far.at[0], False)
    crossed[1].wait_recv()
    crossed[3].wait_recv()
    loads[2].wait()
    add(1, far.at[1], False)
    for h, copy in enumerate(relay):
        copy.wait_recv()
        crossed.append(go(far.at[2, rows[h], :], far.at[2, rows[h], :], twin))
    crossed[4].wait_recv()
    crossed[5].wait_recv()
    loads[3].wait()
    add(2, far.at[2], False)
    part_ref[...] = total[...].astype(BF)
    for copy in done:
        copy.wait_send()


def panel_part(omega, grads):
    vmem = pl.BlockSpec(memory_space=pltpu.VMEM)
    return pl.pallas_call(
        panel_kernel,
        out_shape=jax.ShapeDtypeStruct((LAYERS, ROWS, RANK), BF),
        in_specs=[vmem, pl.BlockSpec(memory_space=pl.ANY)],
        out_specs=vmem,
        scratch_shapes=[
            pltpu.VMEM((NY, LAYERS, ROWS, OWN), BF),
            pltpu.VMEM((NY - 1, OWN, RANK), BF),
            pltpu.VMEM((LAYERS, ROWS, RANK), F32),
            pltpu.SemaphoreType.DMA((2, 12)),
            pltpu.SemaphoreType.DMA((NY,)),
        ],
        compiler_params=pltpu.CompilerParams(collective_id=2, has_side_effects=True, vmem_limit_bytes=48 << 20),
    )(omega, grads)


STREAMS = ((0, 1024), (1024, 1536))
BLOCKS = LAYERS * 10 * B


def rows_at(start, size):
    return pl.ds(pl.multiple_of(start, 8), size)


def gram_kernel(part_ref, panel_ref, blocks_ref, rs_buf, mine, core_buf, chip, x_buf, x_sum, z_buf, strip, y_buf, sems):
    spot = place()
    y, x, z, c = spot
    twin = along("c", spot, 1)
    near_y = [along("y", spot, k) for k in range(1, NY)]
    near_x = [along("x", spot, k) for k in range(1, NX)]
    near_z = [along("z", spot, k) for k in range(1, NZ)]
    greet([twin] + near_y + near_x + near_z)
    done = []
    count = [0]

    def go(src, dst, peer):
        copy = ship(src, dst, sems.at[0, count[0]], sems.at[1, count[0]], peer)
        count[0] += 1
        done.append(copy)
        return copy

    def landed(copies):
        for copy in copies:
            copy.wait_recv()

    q = ROWS // NY
    own = span(y * q, q)
    first = [
        [
            go(part_ref.at[n, span(((y + k) % NY) * q, q), :], rs_buf.at[k - 1, n], near_y[k - 1])
            for k in range(1, NY)
        ]
        for n in range(LAYERS)
    ]
    spread = []
    for n in range(LAYERS):
        landed(first[n])
        total = part_ref[n, own, :].astype(F32)
        for k in range(1, NY):
            total = total + rs_buf[k - 1, n].astype(F32)
        panel_ref[n, own, :] = total.astype(BF)
        whole = panel_ref[n, own, :]
        row = n * 10 * B
        for i in range(4):
            wide = (i + 1) * B
            out = lax.dot_general(whole[:, i * B : wide], whole[:, :wide], TN, preferred_element_type=F32)
            for j in range(i + 1):
                mine[row : row + B, :] = out[:, j * B : j * B + B]
                row += B
        if n == 0:
            start, size = STREAMS[0]
            half = size // 2
            flight = [
                [go(mine.at[rows_at(start + (1 - c) * half, half), :], core_buf.at[pl.ds(start // 2, half), :], twin)]
            ]
    start, size = STREAMS[1]
    half = size // 2
    flight.append(
        [go(mine.at[rows_at(start + (1 - c) * half, half), :], core_buf.at[pl.ds(start // 2, half), :], twin)]
    )

    for s, (start, size) in enumerate(STREAMS):
        half, quarter = size // 2, size // 8
        landed(flight[s])
        here = pl.ds(start // 2, half)
        chip[here, :] = mine[rows_at(start + c * half, half), :] + core_buf[here, :]
        flight[s] = [
            go(
                chip.at[rows_at(start // 2 + ((x + k) % NX) * quarter, quarter), :],
                x_buf.at[k - 1, pl.ds(start // 8, quarter), :],
                near_x[k - 1],
            )
            for k in range(1, NX)
        ]
    for k in range(1, NY):
        spread.append(go(panel_ref.at[:, own, :], panel_ref.at[:, own, :], near_y[k - 1]))
    for s, (start, size) in enumerate(STREAMS):
        quarter, piece = size // 8, size // 64
        landed(flight[s])
        total = chip[rows_at(start // 2 + x * quarter, quarter), :]
        for k in range(1, NX):
            total = total + x_buf[k - 1, start // 8 : start // 8 + quarter, :]
        x_sum[start // 8 : start // 8 + quarter, :] = total
        flight[s] = [
            go(
                x_sum.at[rows_at(start // 8 + ((z + k) % NZ) * piece, piece), :],
                z_buf.at[k - 1, pl.ds(start // 64, piece), :],
                near_z[k - 1],
            )
            for k in range(1, NZ)
        ]
    for s, (start, size) in enumerate(STREAMS):
        piece = size // 64
        landed(flight[s])
        here = pl.ds(start // 64, piece)
        total = x_sum[rows_at(start // 8 + z * piece, piece), :]
        for k in range(1, NZ):
            total = total + z_buf[k - 1, here, :]
        strip[here, :] = total
        flight[s] = [go(strip.at[here, :], y_buf.at[k - 1, here, :], near_y[k - 1]) for k in range(1, NY)]
    for s, (start, size) in enumerate(STREAMS):
        half, quarter, piece = size // 2, size // 8, size // 64
        landed(flight[s])
        here = pl.ds(start // 64, piece)
        total = strip[here, :]
        for k in range(1, NY):
            total = total + y_buf[k - 1, here, :]
        at = rows_at(start + c * half + x * quarter + z * piece, piece)
        blocks_ref[at, :] = total
        flight[s] = [go(blocks_ref.at[at, :], blocks_ref.at[at, :], peer) for peer in near_z]
    for s, (start, size) in enumerate(STREAMS):
        half, quarter = size // 2, size // 8
        landed(flight[s])
        at = rows_at(start + c * half + x * quarter, quarter)
        flight[s] = [go(blocks_ref.at[at, :], blocks_ref.at[at, :], peer) for peer in near_x]
    for s, (start, size) in enumerate(STREAMS):
        half = size // 2
        landed(flight[s])
        at = rows_at(start + c * half, half)
        flight[s] = [go(blocks_ref.at[at, :], blocks_ref.at[at, :], twin)]
    for copies in flight:
        landed(copies)
    landed(spread)
    for copy in done:
        copy.wait_send()


def gram(part):
    vmem = pl.BlockSpec(memory_space=pltpu.VMEM)
    return pl.pallas_call(
        gram_kernel,
        out_shape=(
            jax.ShapeDtypeStruct((LAYERS, ROWS, RANK), BF),
            jax.ShapeDtypeStruct((BLOCKS, B), F32),
        ),
        in_specs=[vmem],
        out_specs=(vmem, vmem),
        scratch_shapes=[
            pltpu.VMEM((NY - 1, LAYERS, ROWS // NY, RANK), BF),
            pltpu.VMEM((BLOCKS, B), F32),
            pltpu.VMEM((BLOCKS // 2, B), F32),
            pltpu.VMEM((BLOCKS // 2, B), F32),
            pltpu.VMEM((NX - 1, BLOCKS // 8, B), F32),
            pltpu.VMEM((BLOCKS // 8, B), F32),
            pltpu.VMEM((NZ - 1, BLOCKS // 64, B), F32),
            pltpu.VMEM((BLOCKS // 64, B), F32),
            pltpu.VMEM((NY - 1, BLOCKS // 64, B), F32),
            pltpu.SemaphoreType.DMA((2, 64)),
        ],
        compiler_params=pltpu.CompilerParams(collective_id=0, has_side_effects=True, vmem_limit_bytes=32 << 20),
    )(part)


def eliminate(tiles):
    lane = lax.broadcasted_iota(jnp.int32, (8, B), 1)
    sub = lax.broadcasted_iota(jnp.int32, (8, B), 0)
    count = B // 8

    def spread(tile, k):
        return jnp.broadcast_to(tile[k : k + 1, :], (8, B))

    def columns(tile, b):
        return [jnp.broadcast_to(tile[:, 8 * b + k : 8 * b + k + 1], (8, B)) for k in range(8)]

    found = [[None] * count for _ in tiles]
    for b in range(count):
        inside = (lane >= 8 * b) & (lane < 8 * b + 8)
        unit = (lane == sub + 8 * b).astype(F32)
        states = []
        for rows in tiles:
            start = jnp.where(inside, unit, rows[b])
            states.append([columns(rows[b], b), start, start, jnp.zeros((8, B), F32)])
        for k in range(8):
            for state in states:
                cols, jordan, forward, scale = state
                pivot = spread(cols[k], k)
                inverse = 1.0 / pivot
                factor = cols[k] * inverse
                for j in range(k + 1, 8):
                    line = spread(cols[j], k)
                    cols[j] = jnp.where(sub == k, line * inverse, cols[j] - factor * line)
                line = spread(jordan, k)
                state[1] = jnp.where(sub == k, line * inverse, jordan - factor * line)
                state[2] = jnp.where(sub > k, forward - factor * spread(forward, k), forward)
                state[3] = jnp.where(sub == k, pivot, scale)
        for n, rows in enumerate(tiles):
            cols, jordan, forward, scale = states[n]
            found[n][b] = jnp.where(lane < 8 * b + 8, forward, 0.0) * lax.rsqrt(scale)
            lines = [spread(jordan, k) for k in range(8)]
            for t in range(b + 1, count):
                cols = columns(rows[t], b)
                terms = [cols[k] * lines[k] for k in range(8)]
                while len(terms) > 1:
                    terms = [terms[i] + terms[i + 1] for i in range(0, len(terms), 2)]
                rows[t] = jnp.where(inside, 0.0, rows[t]) - terms[0]
    return found


def finish(rows):
    return jnp.concatenate(rows, axis=0)


def factor_kernel(blocks_ref, panel_ref, basis_ref, w, inv):
    for n in range(LAYERS):
        row = n * 10 * B
        for i in range(4):
            for j in range(i + 1):
                block = blocks_ref[row : row + B, :]
                row += B
                w[n, i * B : i * B + B, j * B : j * B + B] = block
                if i != j:
                    w[n, j * B : j * B + B, i * B : i * B + B] = block.T

    def step(k, carry):
        here = span(k * B, B)
        tiles = [[w[n, span(k * B + 8 * t, 8), here] for t in range(B // 8)] for n in range(LAYERS)]
        tiles = eliminate(tiles)
        r = lax.broadcasted_iota(jnp.int32, (RANK, 1), 0)
        q = lax.broadcasted_iota(jnp.int32, (1, RANK), 1)
        eye = lax.broadcasted_iota(jnp.int32, (B, RANK), 0) + k * B == lax.broadcasted_iota(jnp.int32, (B, RANK), 1)
        inside = (q >= k * B) & (q < k * B + B)
        below = r >= k * B + B
        for n in range(LAYERS):
            inv[n] = finish(tiles[n])
        for at in range(4):

            @pl.when(k == at)
            def _():
                a, z = at * B, at * B + B
                for n in range(LAYERS):
                    inverse = inv[n]
                    right = jnp.dot(inverse, w[n, a:z, :], precision=HIGHEST, preferred_element_type=F32)
                    pieces = [right[:, :a], inverse, right[:, z:]]
                    right = jnp.concatenate([p for p in pieces if p.shape[1]], axis=1)
                    if z < RANK:
                        left = lax.dot_general(
                            w[n, z:, a:z], inverse, NT, precision=HIGHEST, preferred_element_type=F32
                        )
                        w[n, z:, a:z] = jnp.zeros((RANK - z, B), F32)
                        w[n, z:, :] = w[n, z:, :] - jnp.dot(
                            left, right, precision=HIGHEST, preferred_element_type=F32
                        )
                        right = jnp.concatenate([right[:, :z], jnp.zeros((B, RANK - z), F32)], axis=1)
                    w[n, a:z, :] = right

        return carry

    lax.fori_loop(0, 4, step, 0)
    for n in range(LAYERS):
        rest = w[n]
        basis = jnp.zeros((ROWS, RANK), F32)
        for _ in range(3):
            part = rest.astype(BF)
            rest = rest - part.astype(F32)
            basis = basis + lax.dot_general(panel_ref[n], part, NT, preferred_element_type=F32)
        basis_ref[n] = basis.astype(BF)


def factor(blocks, panel):
    vmem = pl.BlockSpec(memory_space=pltpu.VMEM)
    return pl.pallas_call(
        factor_kernel,
        out_shape=jax.ShapeDtypeStruct((LAYERS, ROWS, RANK), BF),
        in_specs=[vmem, vmem],
        out_specs=vmem,
        scratch_shapes=[pltpu.VMEM((LAYERS, RANK, RANK), F32), pltpu.VMEM((LAYERS, B, B), F32)],
        compiler_params=pltpu.CompilerParams(vmem_limit_bytes=32 << 20),
    )(blocks, panel)


def tail_kernel(
    basis_ref,
    summed_ref,
    first_ref,
    second_ref,
    new_first_ref,
    new_second_ref,
    delta_ref,
    summed,
    twin_basis,
    twin_summed,
    twin_first,
    twin_second,
    back_first,
    back_second,
    relay_out,
    relay_in,
    near_out,
    near_in,
    x_own,
    z_out,
    z_in,
    z_own,
    joined,
    gathered,
    sems,
    local_sems,
):
    spot = place()
    y, x, z, c = spot
    twin = along("c", spot, 1)
    up, down = along("x", spot, 1), along("x", spot, NX - 1)
    near_z = [along("z", spot, k) for k in range(1, NZ)]
    mine, other = span(c * HALF, HALF), span((1 - c) * HALF, HALF)
    loads = []
    for n in range(LAYERS):
        load = pltpu.make_async_copy(summed_ref.at[n, :, mine], summed.at[n], local_sems.at[n])
        load.start()
        loads.append(load)
    greet([twin, up, down] + near_z)
    done = []
    count = [0]

    def go(src, dst, peer):
        copy = ship(src, dst, sems.at[0, count[0]], sems.at[1, count[0]], peer)
        count[0] += 1
        done.append(copy)
        return copy

    def landed(copies):
        for copy in copies:
            copy.wait_recv()

    got = [
        [go(basis_ref.at[n], twin_basis.at[n], twin), go(summed_ref.at[n, :, other], twin_summed.at[n], twin)]
        for n in range(LAYERS)
    ]
    moments = [
        go(first_ref.at[:, :, other], twin_first, twin),
        go(second_ref.at[:, :, other], twin_second, twin),
    ]

    def product(n, start, size):
        here = span(start, size)
        out = lax.dot_general(basis_ref[n, :, here], summed[n], TN, preferred_element_type=F32)
        return out + lax.dot_general(twin_basis[n, :, here], twin_summed[n], TN, preferred_element_type=F32)

    h = B // 2
    above, below, across = ((x + 1) % NX) * B, ((x + NX - 1) % NX) * B, ((x + 2) % NX) * B
    relays, nears = [], []
    for n in range(LAYERS):
        landed(got[n])
        loads[n].wait()
        far = product(n, across, B)
        relay_out[n, 0] = far[:h].astype(BF)
        relay_out[n, 1] = far[h:].astype(BF)
        relays.append([go(relay_out.at[n, 0], relay_in.at[n, 0], up), go(relay_out.at[n, 1], relay_in.at[n, 1], down)])
        x_own[n, 1] = product(n, above, B)
        near_out[n, 0, h:, :] = x_own[n, 1, h:, :].astype(BF)
        copies = [go(near_out.at[n, 0, pl.ds(h, h), :], near_in.at[n, 0, pl.ds(h, h), :], up)]
        x_own[n, 2] = product(n, below, B)
        near_out[n, 1, :h, :] = x_own[n, 2, :h, :].astype(BF)
        copies.append(go(near_out.at[n, 1, pl.ds(0, h), :], near_in.at[n, 1, pl.ds(0, h), :], down))
        nears.append(copies)
        x_own[n, 0] = product(n, x * B, B)
    for n in range(LAYERS):
        relays[n][0].wait_recv()
        near_out[n, 0, :h, :] = (x_own[n, 1, :h, :] + relay_in[n, 0].astype(F32)).astype(BF)
        nears[n].append(go(near_out.at[n, 0, pl.ds(0, h), :], near_in.at[n, 0, pl.ds(0, h), :], up))
        relays[n][1].wait_recv()
        near_out[n, 1, h:, :] = (x_own[n, 2, h:, :] + relay_in[n, 1].astype(F32)).astype(BF)
        nears[n].append(go(near_out.at[n, 1, pl.ds(h, h), :], near_in.at[n, 1, pl.ds(h, h), :], down))

    z_copies = []
    for n in range(LAYERS):
        landed(nears[n])
        total = x_own[n, 0] + near_in[n, 0].astype(F32) + near_in[n, 1].astype(F32)
        x_own[n, 0] = total
        z_out[n] = total.astype(BF)
        z_copies.append(
            [go(z_out.at[n, span(((z + k) % NZ) * 16, 16), :], z_in.at[n, k - 1], near_z[k - 1]) for k in range(1, NZ)]
        )
    landed(moments)
    slot = span(x * B + z * 16, 16)
    ours, theirs = span(c * 8, 8), span((1 - c) * 8, 8)
    spreads = []
    for n in range(LAYERS):
        landed(z_copies[n])
        total = x_own[n, 0, span(z * 16, 16), :]
        for k in range(1, NZ):
            total = total + z_in[n, k - 1].astype(F32)
        z_own[n] = total

        def adam(projected, first, second):
            new_first = 0.9 * first + 0.1 * projected
            new_second = 0.999 * second + 0.001 * projected * projected
            return new_first, new_second, new_first / (jnp.sqrt(new_second) + 1e-08)

        new_first, new_second, fresh = adam(z_own[n, ours, :], first_ref[:, n, mine], second_ref[:, n, mine])
        new_first_ref[:, n, mine] = new_first
        new_second_ref[:, n, mine] = new_second
        joined[n, ours, :] = fresh
        new_first, new_second, fresh = adam(z_own[n, theirs, :], twin_first[:, n, :], twin_second[:, n, :])
        back_first[:, n, :] = new_first
        back_second[:, n, :] = new_second
        joined[n, theirs, :] = fresh
        gathered[c, n, slot, :] = joined[n].astype(BF)
        piece = gathered.at[c, n, slot, :]
        spreads.append([go(piece, piece, peer) for peer in near_z])
    backs = [
        go(back_first, new_first_ref.at[:, :, mine], twin),
        go(back_second, new_second_ref.at[:, :, mine], twin),
    ]

    def part(n, start, size):
        return gathered.at[c, n, pl.ds(pl.multiple_of(start, size), size), :]

    firsts, crossed = [], []
    for n in range(LAYERS):
        landed(spreads[n])
        low, high, whole = part(n, x * B, h), part(n, x * B + h, h), part(n, x * B, B)
        firsts.append([go(low, low, up), go(high, high, down), go(high, high, up), go(low, low, down)])
        crossed.append([go(whole, whole, twin)])
    seconds = []
    for n in range(LAYERS):
        firsts[n][0].wait_recv()
        low = part(n, below, h)
        seconds.append([go(low, low, up)])
        firsts[n][1].wait_recv()
        high = part(n, above + h, h)
        seconds[n].append(go(high, high, down))
        landed(firsts[n][2:])
        for start in (below, above):
            whole = part(n, start, B)
            crossed[n].append(go(whole, whole, twin))
    tile = 256
    for n in range(LAYERS):
        landed(seconds[n])
        whole = part(n, across, B)
        crossed[n].append(go(whole, whole, twin))

        def make(half):
            def body(t, carry):
                right = gathered[half, n, :, span(t * tile, tile)]
                out = jnp.dot(basis_ref[n], right, preferred_element_type=F32)
                delta_ref[n, :, pl.ds(pl.multiple_of(half * HALF + t * tile, tile), tile)] = out.astype(BF)
                return carry

            lax.fori_loop(0, HALF // tile, body, 0)

        make(c)
        landed(crossed[n])
        make(1 - c)
    landed(backs)
    for copy in done:
        copy.wait_send()


def tail(basis, summed, first, second):
    vmem = pl.BlockSpec(memory_space=pltpu.VMEM)
    return pl.pallas_call(
        tail_kernel,
        out_shape=(
            jax.ShapeDtypeStruct((8, LAYERS, OWN), F32),
            jax.ShapeDtypeStruct((8, LAYERS, OWN), F32),
            jax.ShapeDtypeStruct((LAYERS, ROWS, OWN), BF),
        ),
        in_specs=[vmem, pl.BlockSpec(memory_space=pl.ANY), vmem, vmem],
        out_specs=(vmem,) * 3,
        scratch_shapes=[
            pltpu.VMEM((LAYERS, ROWS, HALF), BF),
            pltpu.VMEM((LAYERS, ROWS, RANK), BF),
            pltpu.VMEM((LAYERS, ROWS, HALF), BF),
            pltpu.VMEM((8, LAYERS, HALF), F32),
            pltpu.VMEM((8, LAYERS, HALF), F32),
            pltpu.VMEM((8, LAYERS, HALF), F32),
            pltpu.VMEM((8, LAYERS, HALF), F32),
            pltpu.VMEM((LAYERS, 2, B // 2, HALF), BF),
            pltpu.VMEM((LAYERS, 2, B // 2, HALF), BF),
            pltpu.VMEM((LAYERS, 2, B, HALF), BF),
            pltpu.VMEM((LAYERS, 2, B, HALF), BF),
            pltpu.VMEM((LAYERS, 3, B, HALF), F32),
            pltpu.VMEM((LAYERS, B, HALF), BF),
            pltpu.VMEM((LAYERS, NZ - 1, 16, HALF), BF),
            pltpu.VMEM((LAYERS, 16, HALF), F32),
            pltpu.VMEM((LAYERS, 16, HALF), F32),
            pltpu.VMEM((2, LAYERS, RANK, HALF), BF),
            pltpu.SemaphoreType.DMA((2, 80)),
            pltpu.SemaphoreType.DMA((LAYERS,)),
        ],
        compiler_params=pltpu.CompilerParams(collective_id=1, has_side_effects=True, vmem_limit_bytes=48 << 20),
    )(basis, summed, first, second)


def local(grad_parts, omega, first_moment, second_moment):
    part = panel_part(omega, grad_parts[0])
    grads, part = lax.optimization_barrier((grad_parts[0], part))
    summed = lax.psum_scatter(grads, "dp", scatter_dimension=2, tiled=True)
    panel, blocks = gram(part)
    basis = factor(blocks, panel)
    return tail(basis, summed, first_moment, second_moment)


def solution(mesh):
    return jax.shard_map(
        local,
        mesh=mesh,
        in_specs=(P("dp", None, "mp", None), P("dp", None), P("mp", None, "dp"), P("mp", None, "dp")),
        out_specs=(P("mp", None, "dp"), P("mp", None, "dp"), P(None, "mp", "dp")),
        check_vma=False,
    )
```

```python
import functools

import jax
import jax.numpy as jnp
from jax import lax
from jax.experimental import pallas as pl
from jax.experimental.pallas import tpu as pltpu
from jax.sharding import PartitionSpec as P

HIGHEST = lax.Precision.HIGHEST
MESH = pl.DeviceIdType.MESH
NT = (((1,), (1,)), ((), ()))
TN = (((0,), (0,)), ((), ()))
BF = jnp.bfloat16
F32 = jnp.float32

LAYERS = 2
ROWS = 256
D = 8192
OWN = 2048
HALF = 1024
RANK = 512
B = 128
NY, NX, NZ, NC = 4, 4, 8, 2


def place():
    mp = lax.axis_index("mp")
    return lax.axis_index("dp"), mp // (NZ * NC), (mp // NC) % NZ, mp % NC


def device(y, x, z, c):
    return {"dp": y, "mp": x * (NZ * NC) + z * NC + c}


def greet(peers):
    barrier = pltpu.get_barrier_semaphore()
    for peer in peers:
        pl.semaphore_signal(barrier, inc=1, device_id=peer, device_id_type=MESH)
    pl.semaphore_wait(barrier, len(peers))


def along(axis, spot, k):
    y, x, z, c = spot
    if axis == "y":
        return device((y + k) % NY, x, z, c)
    if axis == "x":
        return device(y, (x + k) % NX, z, c)
    if axis == "z":
        return device(y, x, (z + k) % NZ, c)
    return device(y, x, z, 1 - c)


def ship(src, dst, send, recv, peer):
    copy = pltpu.make_async_remote_copy(
        src_ref=src, dst_ref=dst, send_sem=send, recv_sem=recv, device_id=peer, device_id_type=MESH
    )
    copy.start()
    return copy


def span(start, size):
    return pl.ds(pl.multiple_of(start, size), size)


STREAMS = ((0, 1024), (1024, 1536))
BLOCKS = LAYERS * 10 * B
FAR = NY - 1


def rows_at(start, size):
    return pl.ds(pl.multiple_of(start, 8), size)


def front_kernel(
    omega_hbm,
    grads_hbm,
    summed_ref,
    panel_ref,
    blocks_ref,
    omega_ref,
    grads,
    omegas,
    relay_in,
    joint,
    near_in,
    partial,
    part,
    rs_buf,
    mine,
    core_buf,
    chip,
    x_buf,
    x_sum,
    z_buf,
    strip,
    y_buf,
    sems,
    local_sems,
):
    spot = place()
    y, x, z, c = spot
    twin = along("c", spot, 1)
    near_y = [along("y", spot, k) for k in range(1, NY)]
    near_x = [along("x", spot, k) for k in range(1, NX)]
    near_z = [along("z", spot, k) for k in range(1, NZ)]
    loads = [pltpu.make_async_copy(omega_hbm, omega_ref, local_sems.at[NY])]
    loads[0].start()
    for k in (0, 1, 3, 2):
        columns = span(((y + k) % NY) * OWN, OWN)
        load = pltpu.make_async_copy(grads_hbm.at[:, :, columns], grads.at[k], local_sems.at[k])
        load.start()
        loads.append(load)
    greet([twin] + near_y + near_x + near_z)
    done = []
    count = [0]

    def go(src, dst, peer):
        copy = ship(src, dst, sems.at[0, count[0]], sems.at[1, count[0]], peer)
        count[0] += 1
        done.append(copy)
        return copy

    def landed(copies):
        for copy in copies:
            copy.wait_recv()

    relays, nears = [None] * 2, [None] * 2

    def launch(part_of):
        off = (1 - part_of) * HALF

        def columns(k):
            return span(((y + k) % NY) * OWN + off, HALF)

        relays[part_of] = [
            go(grads_hbm.at[0, :, columns(2)], relay_in.at[part_of, 0], near_y[0]),
            go(grads_hbm.at[1, :, columns(2)], relay_in.at[part_of, 1], near_y[2]),
        ]
        nears[part_of] = [
            go(grads_hbm.at[1, :, columns(1)], near_in.at[part_of, 0, 1], near_y[0]),
            go(grads_hbm.at[0, :, columns(3)], near_in.at[part_of, 1, 0], near_y[2]),
        ]

    def in_rows(work):
        def body(t, carry):
            work(span(t * 32, 32))
            return carry

        lax.fori_loop(0, ROWS // 32, body, 0)

    def combine(part_of):
        off = (1 - part_of) * HALF
        for n, k in ((0, 1), (1, 3)):
            relays[part_of][n].wait_recv()

            def work(at):
                own_term = grads[k, n, at, off : off + HALF].astype(F32)
                joint[part_of, n, at, :] = (own_term + relay_in[part_of, n, at, :].astype(F32)).astype(BF)

            in_rows(work)
            nears[part_of].append(go(joint.at[part_of, n], near_in.at[part_of, n, n], near_y[k - 1]))

    def finish_sum(part_of):
        off = (1 - part_of) * HALF
        landed(nears[part_of])

        def work(at):
            for n in range(LAYERS):
                out = grads[0, n, at, off : off + HALF].astype(F32) + near_in[part_of, 0, n, at, :].astype(F32)
                summed_ref[n, at, off : off + HALF] = (out + near_in[part_of, 1, n, at, :].astype(F32)).astype(BF)

        in_rows(work)

    strip_at = span(x * 256 + c * B + z * 16, 16)
    slices = [go(omega_hbm.at[strip_at, :], omegas.at[FAR - k, strip_at, :], near_y[k - 1]) for k in range(1, NY)]
    launch(0)

    def block(s, which, start, size):
        return omegas.at[s, pl.ds(pl.multiple_of(which * 256 + c * B + start, size), size), :]

    flights = []
    for s in range(FAR):
        slices[FAR - 1 - s].wait_recv()
        piece = omegas.at[s, strip_at, :]
        flights.append([go(piece, piece, peer) for peer in near_z])
    for load in loads:
        load.wait()
    for n in range(LAYERS):
        partial[n] = jnp.dot(grads[0, n, :, :HALF], omega_ref[:HALF, :], preferred_element_type=F32)
    up, down = near_x[0], near_x[2]
    above, below, across = (x + 1) % NX, (x + NX - 1) % NX, (x + 2) % NX
    h = B // 2
    firsts, crossed, seconds = [], [], []
    for s in range(FAR):
        landed(flights[s])
        low, high, whole = block(s, x, 0, h), block(s, x, h, h), block(s, x, 0, B)
        firsts.append([go(low, low, up), go(high, high, down), go(high, high, up), go(low, low, down)])
        crossed.append([go(whole, whole, twin)])
    combine(0)
    for s in range(FAR):
        firsts[s][0].wait_recv()
        low = block(s, below, 0, h)
        seconds.append([go(low, low, up)])
        firsts[s][1].wait_recv()
        high = block(s, above, h, h)
        seconds[s].append(go(high, high, down))
        landed(firsts[s][2:])
        for which in (below, above):
            whole = block(s, which, 0, B)
            crossed[s].append(go(whole, whole, twin))
    for s in range(FAR):
        landed(seconds[s])
        whole = block(s, across, 0, B)
        crossed[s].append(go(whole, whole, twin))
    for s in range(FAR):
        landed(crossed[s])
        for n in range(LAYERS):
            partial[n] += jnp.dot(grads[s + 1, n, :, :HALF], omegas[s], preferred_element_type=F32)
    finish_sum(0)
    for n in range(LAYERS):
        out = partial[n] + jnp.dot(summed_ref[n, :, HALF:], omega_ref[HALF:, :], preferred_element_type=F32)
        part[n] = out.astype(BF)

    q = ROWS // NY
    own = span(y * q, q)
    first = [
        [
            go(part.at[n, span(((y + k) % NY) * q, q), :], rs_buf.at[k - 1, n], near_y[k - 1])
            for k in range(1, NY)
        ]
        for n in range(LAYERS)
    ]
    spread = []
    for n in range(LAYERS):
        landed(first[n])
        if n == 1:
            launch(1)
        total = part[n, own, :].astype(F32)
        for k in range(1, NY):
            total = total + rs_buf[k - 1, n].astype(F32)
        panel_ref[n, own, :] = total.astype(BF)
        whole = panel_ref[n, own, :]
        row = n * 10 * B
        for i in range(4):
            wide = (i + 1) * B
            out = lax.dot_general(whole[:, i * B : wide], whole[:, :wide], TN, preferred_element_type=F32)
            for j in range(i + 1):
                mine[row : row + B, :] = out[:, j * B : j * B + B]
                row += B
        if n == 0:
            start, size = STREAMS[0]
            half = size // 2
            flight = [
                [go(mine.at[rows_at(start + (1 - c) * half, half), :], core_buf.at[pl.ds(start // 2, half), :], twin)]
            ]
    start, size = STREAMS[1]
    half = size // 2
    flight.append(
        [go(mine.at[rows_at(start + (1 - c) * half, half), :], core_buf.at[pl.ds(start // 2, half), :], twin)]
    )

    for s, (start, size) in enumerate(STREAMS):
        half, quarter = size // 2, size // 8
        landed(flight[s])
        here = pl.ds(start // 2, half)
        chip[here, :] = mine[rows_at(start + c * half, half), :] + core_buf[here, :]
        flight[s] = [
            go(
                chip.at[rows_at(start // 2 + ((x + k) % NX) * quarter, quarter), :],
                x_buf.at[k - 1, pl.ds(start // 8, quarter), :],
                near_x[k - 1],
            )
            for k in range(1, NX)
        ]
    for k in range(1, NY):
        spread.append(go(panel_ref.at[:, own, :], panel_ref.at[:, own, :], near_y[k - 1]))
    for s, (start, size) in enumerate(STREAMS):
        quarter, piece = size // 8, size // 64
        landed(flight[s])
        total = chip[rows_at(start // 2 + x * quarter, quarter), :]
        for k in range(1, NX):
            total = total + x_buf[k - 1, start // 8 : start // 8 + quarter, :]
        x_sum[start // 8 : start // 8 + quarter, :] = total
        flight[s] = [
            go(
                x_sum.at[rows_at(start // 8 + ((z + k) % NZ) * piece, piece), :],
                z_buf.at[k - 1, pl.ds(start // 64, piece), :],
                near_z[k - 1],
            )
            for k in range(1, NZ)
        ]
    combine(1)
    for s, (start, size) in enumerate(STREAMS):
        piece = size // 64
        landed(flight[s])
        here = pl.ds(start // 64, piece)
        total = x_sum[rows_at(start // 8 + z * piece, piece), :]
        for k in range(1, NZ):
            total = total + z_buf[k - 1, here, :]
        strip[here, :] = total
        flight[s] = [go(strip.at[here, :], y_buf.at[k - 1, here, :], near_y[k - 1]) for k in range(1, NY)]
    for s, (start, size) in enumerate(STREAMS):
        half, quarter, piece = size // 2, size // 8, size // 64
        landed(flight[s])
        here = pl.ds(start // 64, piece)
        total = strip[here, :]
        for k in range(1, NY):
            total = total + y_buf[k - 1, here, :]
        at = rows_at(start + c * half + x * quarter + z * piece, piece)
        blocks_ref[at, :] = total
        flight[s] = [go(blocks_ref.at[at, :], blocks_ref.at[at, :], peer) for peer in near_z]
    for s, (start, size) in enumerate(STREAMS):
        half, quarter = size // 2, size // 8
        landed(flight[s])
        at = rows_at(start + c * half + x * quarter, quarter)
        flight[s] = [go(blocks_ref.at[at, :], blocks_ref.at[at, :], peer) for peer in near_x]
    for s, (start, size) in enumerate(STREAMS):
        half = size // 2
        landed(flight[s])
        at = rows_at(start + c * half, half)
        flight[s] = [go(blocks_ref.at[at, :], blocks_ref.at[at, :], twin)]
    finish_sum(1)
    for copies in flight:
        landed(copies)
    landed(spread)
    for copy in done:
        copy.wait_send()


def front(omega, grads):
    vmem = pl.BlockSpec(memory_space=pltpu.VMEM)
    return pl.pallas_call(
        front_kernel,
        out_shape=(
            jax.ShapeDtypeStruct((LAYERS, ROWS, OWN), BF),
            jax.ShapeDtypeStruct((LAYERS, ROWS, RANK), BF),
            jax.ShapeDtypeStruct((BLOCKS, B), F32),
        ),
        in_specs=[pl.BlockSpec(memory_space=pl.ANY)] * 2,
        out_specs=(vmem, vmem, vmem),
        scratch_shapes=[
            pltpu.VMEM((OWN, RANK), BF),
            pltpu.VMEM((NY, LAYERS, ROWS, OWN), BF),
            pltpu.VMEM((FAR, HALF, RANK), BF),
            pltpu.VMEM((2, LAYERS, ROWS, HALF), BF),
            pltpu.VMEM((2, LAYERS, ROWS, HALF), BF),
            pltpu.VMEM((2, 2, LAYERS, ROWS, HALF), BF),
            pltpu.VMEM((LAYERS, ROWS, RANK), F32),
            pltpu.VMEM((LAYERS, ROWS, RANK), BF),
            pltpu.VMEM((NY - 1, LAYERS, ROWS // NY, RANK), BF),
            pltpu.VMEM((BLOCKS, B), F32),
            pltpu.VMEM((BLOCKS // 2, B), F32),
            pltpu.VMEM((BLOCKS // 2, B), F32),
            pltpu.VMEM((NX - 1, BLOCKS // 8, B), F32),
            pltpu.VMEM((BLOCKS // 8, B), F32),
            pltpu.VMEM((NZ - 1, BLOCKS // 64, B), F32),
            pltpu.VMEM((BLOCKS // 64, B), F32),
            pltpu.VMEM((NY - 1, BLOCKS // 64, B), F32),
            pltpu.SemaphoreType.DMA((2, 160)),
            pltpu.SemaphoreType.DMA((NY + 1,)),
        ],
        compiler_params=pltpu.CompilerParams(collective_id=0, has_side_effects=True, vmem_limit_bytes=36 << 20),
    )(omega, grads)


def eliminate(tiles):
    lane = lax.broadcasted_iota(jnp.int32, (8, B), 1)
    sub = lax.broadcasted_iota(jnp.int32, (8, B), 0)
    count = B // 8

    def spread(tile, k):
        return jnp.broadcast_to(tile[k : k + 1, :], (8, B))

    def columns(tile, b):
        return [jnp.broadcast_to(tile[:, 8 * b + k : 8 * b + k + 1], (8, B)) for k in range(8)]

    found = [[None] * count for _ in tiles]
    for b in range(count):
        inside = (lane >= 8 * b) & (lane < 8 * b + 8)
        unit = (lane == sub + 8 * b).astype(F32)
        states = []
        for rows in tiles:
            start = jnp.where(inside, unit, rows[b])
            states.append([columns(rows[b], b), start, start, jnp.zeros((8, B), F32)])
        for k in range(8):
            for state in states:
                cols, jordan, forward, scale = state
                pivot = spread(cols[k], k)
                inverse = 1.0 / pivot
                factor = cols[k] * inverse
                for j in range(k + 1, 8):
                    line = spread(cols[j], k)
                    cols[j] = jnp.where(sub == k, line * inverse, cols[j] - factor * line)
                line = spread(jordan, k)
                state[1] = jnp.where(sub == k, line * inverse, jordan - factor * line)
                state[2] = jnp.where(sub > k, forward - factor * spread(forward, k), forward)
                state[3] = jnp.where(sub == k, pivot, scale)
        for n, rows in enumerate(tiles):
            cols, jordan, forward, scale = states[n]
            found[n][b] = jnp.where(lane < 8 * b + 8, forward, 0.0) * lax.rsqrt(scale)
            lines = [spread(jordan, k) for k in range(8)]
            for t in range(b + 1, count):
                cols = columns(rows[t], b)
                terms = [cols[k] * lines[k] for k in range(8)]
                while len(terms) > 1:
                    terms = [terms[i] + terms[i + 1] for i in range(0, len(terms), 2)]
                rows[t] = jnp.where(inside, 0.0, rows[t]) - terms[0]
    return found


def finish(rows):
    return jnp.concatenate(rows, axis=0)


def factor_kernel(blocks_ref, panel_ref, basis_ref, w, inv):
    for n in range(LAYERS):
        row = n * 10 * B
        for i in range(4):
            for j in range(i + 1):
                block = blocks_ref[row : row + B, :]
                row += B
                w[n, i * B : i * B + B, j * B : j * B + B] = block
                if i != j:
                    w[n, j * B : j * B + B, i * B : i * B + B] = block.T

    def step(k, carry):
        here = span(k * B, B)
        tiles = [[w[n, span(k * B + 8 * t, 8), here] for t in range(B // 8)] for n in range(LAYERS)]
        tiles = eliminate(tiles)
        r = lax.broadcasted_iota(jnp.int32, (RANK, 1), 0)
        q = lax.broadcasted_iota(jnp.int32, (1, RANK), 1)
        eye = lax.broadcasted_iota(jnp.int32, (B, RANK), 0) + k * B == lax.broadcasted_iota(jnp.int32, (B, RANK), 1)
        inside = (q >= k * B) & (q < k * B + B)
        below = r >= k * B + B
        for n in range(LAYERS):
            inv[n] = finish(tiles[n])
        for at in range(4):

            @pl.when(k == at)
            def _():
                a, z = at * B, at * B + B
                for n in range(LAYERS):
                    inverse = inv[n]
                    right = jnp.dot(inverse, w[n, a:z, :], precision=HIGHEST, preferred_element_type=F32)
                    pieces = [right[:, :a], inverse, right[:, z:]]
                    right = jnp.concatenate([p for p in pieces if p.shape[1]], axis=1)
                    if z < RANK:
                        left = lax.dot_general(
                            w[n, z:, a:z], inverse, NT, precision=HIGHEST, preferred_element_type=F32
                        )
                        w[n, z:, a:z] = jnp.zeros((RANK - z, B), F32)
                        w[n, z:, :] = w[n, z:, :] - jnp.dot(
                            left, right, precision=HIGHEST, preferred_element_type=F32
                        )
                        right = jnp.concatenate([right[:, :z], jnp.zeros((B, RANK - z), F32)], axis=1)
                    w[n, a:z, :] = right

        return carry

    lax.fori_loop(0, 4, step, 0)
    for n in range(LAYERS):
        rest = w[n]
        basis = jnp.zeros((ROWS, RANK), F32)
        for _ in range(3):
            part = rest.astype(BF)
            rest = rest - part.astype(F32)
            basis = basis + lax.dot_general(panel_ref[n], part, NT, preferred_element_type=F32)
        basis_ref[n] = basis.astype(BF)


def factor(blocks, panel):
    vmem = pl.BlockSpec(memory_space=pltpu.VMEM)
    return pl.pallas_call(
        factor_kernel,
        out_shape=jax.ShapeDtypeStruct((LAYERS, ROWS, RANK), BF),
        in_specs=[vmem, vmem],
        out_specs=vmem,
        scratch_shapes=[pltpu.VMEM((LAYERS, RANK, RANK), F32), pltpu.VMEM((LAYERS, B, B), F32)],
        compiler_params=pltpu.CompilerParams(vmem_limit_bytes=32 << 20),
    )(blocks, panel)


def tail_kernel(
    basis_ref,
    summed_ref,
    first_ref,
    second_ref,
    new_first_ref,
    new_second_ref,
    delta_ref,
    summed,
    twin_basis,
    twin_summed,
    twin_first,
    twin_second,
    back_first,
    back_second,
    relay_out,
    relay_in,
    near_out,
    near_in,
    x_own,
    z_out,
    z_in,
    z_own,
    joined,
    gathered,
    sems,
    local_sems,
):
    spot = place()
    y, x, z, c = spot
    twin = along("c", spot, 1)
    up, down = along("x", spot, 1), along("x", spot, NX - 1)
    near_z = [along("z", spot, k) for k in range(1, NZ)]
    mine, other = span(c * HALF, HALF), span((1 - c) * HALF, HALF)
    loads = []
    for n in range(LAYERS):
        load = pltpu.make_async_copy(summed_ref.at[n, :, mine], summed.at[n], local_sems.at[n])
        load.start()
        loads.append(load)
    greet([twin, up, down] + near_z)
    done = []
    count = [0]

    def go(src, dst, peer):
        copy = ship(src, dst, sems.at[0, count[0]], sems.at[1, count[0]], peer)
        count[0] += 1
        done.append(copy)
        return copy

    def landed(copies):
        for copy in copies:
            copy.wait_recv()

    got = [
        [go(basis_ref.at[n], twin_basis.at[n], twin), go(summed_ref.at[n, :, other], twin_summed.at[n], twin)]
        for n in range(LAYERS)
    ]
    moments = [
        go(first_ref.at[:, :, other], twin_first, twin),
        go(second_ref.at[:, :, other], twin_second, twin),
    ]

    def product(n, start, size):
        here = span(start, size)
        out = lax.dot_general(basis_ref[n, :, here], summed[n], TN, preferred_element_type=F32)
        return out + lax.dot_general(twin_basis[n, :, here], twin_summed[n], TN, preferred_element_type=F32)

    h = B // 2
    above, below, across = ((x + 1) % NX) * B, ((x + NX - 1) % NX) * B, ((x + 2) % NX) * B
    relays, nears = [], []
    for n in range(LAYERS):
        landed(got[n])
        loads[n].wait()
        far = product(n, across, B)
        relay_out[n, 0] = far[:h].astype(BF)
        relay_out[n, 1] = far[h:].astype(BF)
        relays.append([go(relay_out.at[n, 0], relay_in.at[n, 0], up), go(relay_out.at[n, 1], relay_in.at[n, 1], down)])
        x_own[n, 1] = product(n, above, B)
        near_out[n, 0, h:, :] = x_own[n, 1, h:, :].astype(BF)
        copies = [go(near_out.at[n, 0, pl.ds(h, h), :], near_in.at[n, 0, pl.ds(h, h), :], up)]
        x_own[n, 2] = product(n, below, B)
        near_out[n, 1, :h, :] = x_own[n, 2, :h, :].astype(BF)
        copies.append(go(near_out.at[n, 1, pl.ds(0, h), :], near_in.at[n, 1, pl.ds(0, h), :], down))
        nears.append(copies)
        x_own[n, 0] = product(n, x * B, B)
    for n in range(LAYERS):
        relays[n][0].wait_recv()
        near_out[n, 0, :h, :] = (x_own[n, 1, :h, :] + relay_in[n, 0].astype(F32)).astype(BF)
        nears[n].append(go(near_out.at[n, 0, pl.ds(0, h), :], near_in.at[n, 0, pl.ds(0, h), :], up))
        relays[n][1].wait_recv()
        near_out[n, 1, h:, :] = (x_own[n, 2, h:, :] + relay_in[n, 1].astype(F32)).astype(BF)
        nears[n].append(go(near_out.at[n, 1, pl.ds(h, h), :], near_in.at[n, 1, pl.ds(h, h), :], down))

    z_copies = []
    for n in range(LAYERS):
        landed(nears[n])
        total = x_own[n, 0] + near_in[n, 0].astype(F32) + near_in[n, 1].astype(F32)
        x_own[n, 0] = total
        z_out[n] = total.astype(BF)
        z_copies.append(
            [go(z_out.at[n, span(((z + k) % NZ) * 16, 16), :], z_in.at[n, k - 1], near_z[k - 1]) for k in range(1, NZ)]
        )
    landed(moments)
    slot = span(x * B + z * 16, 16)
    ours, theirs = span(c * 8, 8), span((1 - c) * 8, 8)
    spreads = []
    for n in range(LAYERS):
        landed(z_copies[n])
        total = x_own[n, 0, span(z * 16, 16), :]
        for k in range(1, NZ):
            total = total + z_in[n, k - 1].astype(F32)
        z_own[n] = total

        def adam(projected, first, second):
            new_first = 0.9 * first + 0.1 * projected
            new_second = 0.999 * second + 0.001 * projected * projected
            return new_first, new_second, new_first / (jnp.sqrt(new_second) + 1e-08)

        new_first, new_second, fresh = adam(z_own[n, ours, :], first_ref[:, n, mine], second_ref[:, n, mine])
        new_first_ref[:, n, mine] = new_first
        new_second_ref[:, n, mine] = new_second
        joined[n, ours, :] = fresh
        new_first, new_second, fresh = adam(z_own[n, theirs, :], twin_first[:, n, :], twin_second[:, n, :])
        back_first[:, n, :] = new_first
        back_second[:, n, :] = new_second
        joined[n, theirs, :] = fresh
        gathered[c, n, slot, :] = joined[n].astype(BF)
        piece = gathered.at[c, n, slot, :]
        spreads.append([go(piece, piece, peer) for peer in near_z])
    backs = [
        go(back_first, new_first_ref.at[:, :, mine], twin),
        go(back_second, new_second_ref.at[:, :, mine], twin),
    ]

    def part(n, start, size):
        return gathered.at[c, n, pl.ds(pl.multiple_of(start, size), size), :]

    firsts, crossed = [], []
    for n in range(LAYERS):
        landed(spreads[n])
        low, high, whole = part(n, x * B, h), part(n, x * B + h, h), part(n, x * B, B)
        firsts.append([go(low, low, up), go(high, high, down), go(high, high, up), go(low, low, down)])
        crossed.append([go(whole, whole, twin)])
    seconds = []
    for n in range(LAYERS):
        firsts[n][0].wait_recv()
        low = part(n, below, h)
        seconds.append([go(low, low, up)])
        firsts[n][1].wait_recv()
        high = part(n, above + h, h)
        seconds[n].append(go(high, high, down))
        landed(firsts[n][2:])
        for start in (below, above):
            whole = part(n, start, B)
            crossed[n].append(go(whole, whole, twin))
    tile = 256
    for n in range(LAYERS):
        landed(seconds[n])
        whole = part(n, across, B)
        crossed[n].append(go(whole, whole, twin))

        def make(half):
            def body(t, carry):
                right = gathered[half, n, :, span(t * tile, tile)]
                out = jnp.dot(basis_ref[n], right, preferred_element_type=F32)
                delta_ref[n, :, pl.ds(pl.multiple_of(half * HALF + t * tile, tile), tile)] = out.astype(BF)
                return carry

            lax.fori_loop(0, HALF // tile, body, 0)

        make(c)
        landed(crossed[n])
        make(1 - c)
    landed(backs)
    for copy in done:
        copy.wait_send()


def tail(basis, summed, first, second):
    vmem = pl.BlockSpec(memory_space=pltpu.VMEM)
    return pl.pallas_call(
        tail_kernel,
        out_shape=(
            jax.ShapeDtypeStruct((8, LAYERS, OWN), F32),
            jax.ShapeDtypeStruct((8, LAYERS, OWN), F32),
            jax.ShapeDtypeStruct((LAYERS, ROWS, OWN), BF),
        ),
        in_specs=[vmem, pl.BlockSpec(memory_space=pl.ANY), vmem, vmem],
        out_specs=(vmem,) * 3,
        scratch_shapes=[
            pltpu.VMEM((LAYERS, ROWS, HALF), BF),
            pltpu.VMEM((LAYERS, ROWS, RANK), BF),
            pltpu.VMEM((LAYERS, ROWS, HALF), BF),
            pltpu.VMEM((8, LAYERS, HALF), F32),
            pltpu.VMEM((8, LAYERS, HALF), F32),
            pltpu.VMEM((8, LAYERS, HALF), F32),
            pltpu.VMEM((8, LAYERS, HALF), F32),
            pltpu.VMEM((LAYERS, 2, B // 2, HALF), BF),
            pltpu.VMEM((LAYERS, 2, B // 2, HALF), BF),
            pltpu.VMEM((LAYERS, 2, B, HALF), BF),
            pltpu.VMEM((LAYERS, 2, B, HALF), BF),
            pltpu.VMEM((LAYERS, 3, B, HALF), F32),
            pltpu.VMEM((LAYERS, B, HALF), BF),
            pltpu.VMEM((LAYERS, NZ - 1, 16, HALF), BF),
            pltpu.VMEM((LAYERS, 16, HALF), F32),
            pltpu.VMEM((LAYERS, 16, HALF), F32),
            pltpu.VMEM((2, LAYERS, RANK, HALF), BF),
            pltpu.SemaphoreType.DMA((2, 80)),
            pltpu.SemaphoreType.DMA((LAYERS,)),
        ],
        compiler_params=pltpu.CompilerParams(collective_id=1, has_side_effects=True, vmem_limit_bytes=48 << 20),
    )(basis, summed, first, second)


def local(grad_parts, omega, first_moment, second_moment):
    summed, panel, blocks = front(omega, grad_parts[0])
    basis = factor(blocks, panel)
    return tail(basis, summed, first_moment, second_moment)


def solution(mesh):
    return jax.shard_map(
        local,
        mesh=mesh,
        in_specs=(P("dp", None, "mp", None), P("dp", None), P("mp", None, "dp"), P("mp", None, "dp")),
        out_specs=(P("mp", None, "dp"), P("mp", None, "dp"), P(None, "mp", "dp")),
        check_vma=False,
    )
```

```python
import functools

import jax
import jax.numpy as jnp
from jax import lax
from jax.experimental import pallas as pl
from jax.experimental.pallas import tpu as pltpu
from jax.sharding import PartitionSpec as P

HIGHEST = lax.Precision.HIGHEST
MESH = pl.DeviceIdType.MESH
NT = (((1,), (1,)), ((), ()))
TN = (((0,), (0,)), ((), ()))
BF = jnp.bfloat16
F32 = jnp.float32

LAYERS = 2
ROWS = 256
D = 8192
OWN = 2048
HALF = 1024
RANK = 512
B = 128
NY, NX, NZ, NC = 4, 4, 8, 2


def place():
    mp = lax.axis_index("mp")
    return lax.axis_index("dp"), mp // (NZ * NC), (mp // NC) % NZ, mp % NC


def device(y, x, z, c):
    return {"dp": y, "mp": x * (NZ * NC) + z * NC + c}


def greet(peers):
    barrier = pltpu.get_barrier_semaphore()
    for peer in peers:
        pl.semaphore_signal(barrier, inc=1, device_id=peer, device_id_type=MESH)
    pl.semaphore_wait(barrier, len(peers))


def along(axis, spot, k):
    y, x, z, c = spot
    if axis == "y":
        return device((y + k) % NY, x, z, c)
    if axis == "x":
        return device(y, (x + k) % NX, z, c)
    if axis == "z":
        return device(y, x, (z + k) % NZ, c)
    return device(y, x, z, 1 - c)


def ship(src, dst, send, recv, peer):
    copy = pltpu.make_async_remote_copy(
        src_ref=src, dst_ref=dst, send_sem=send, recv_sem=recv, device_id=peer, device_id_type=MESH
    )
    copy.start()
    return copy


def span(start, size):
    return pl.ds(pl.multiple_of(start, size), size)


def eliminate(whole):
    lane = lax.broadcasted_iota(jnp.int32, (1, 8, B), 2)
    sub = lax.broadcasted_iota(jnp.int32, (1, 8, B), 1)
    sub4 = lax.broadcasted_iota(jnp.int32, (1, 1, 8, B), 2)
    found = []
    for b in range(B // 8):
        inside = (lane >= 8 * b) & (lane < 8 * b + 8)
        top = whole[:, :8, :]
        cols = [top[:, :, 8 * b + k : 8 * b + k + 1] for k in range(8)]
        cols = jnp.stack([jnp.broadcast_to(col, (LAYERS, 8, B)) for col in cols], axis=1)
        start = jnp.where(inside, (lane == sub + 8 * b).astype(F32), top)
        state = jnp.concatenate([cols, start[:, None]], axis=1)
        forward = start
        scale = jnp.zeros((LAYERS, 8, B), F32)
        for k in range(8):
            column = state[:, k]
            pivot = column[:, k : k + 1, :]
            inverse = 1.0 / pivot
            factor = column * inverse
            line = state[:, :, k : k + 1, :]
            state = jnp.where(sub4 == k, line * inverse[:, None], state - factor[:, None] * line)
            forward = jnp.where(sub > k, forward - factor * forward[:, k : k + 1, :], forward)
            scale = jnp.where(sub == k, pivot, scale)
        found.append(jnp.where(lane < 8 * b + 8, forward, 0.0) * lax.rsqrt(scale))
        if b < B // 8 - 1:
            rest = whole[:, 8:, :]
            total = None
            for k in range(8):
                term = rest[:, :, 8 * b + k : 8 * b + k + 1] * state[:, 8, k : k + 1, :]
                total = term if total is None else total + term
            whole = jnp.where(inside[:, :1], 0.0, rest) - total
    return jnp.concatenate(found, axis=1)


STREAMS = ((0, 1024), (1024, 1536))
BLOCKS = LAYERS * 10 * B
FAR = NY - 1


def rows_at(start, size):
    return pl.ds(pl.multiple_of(start, 8), size)


def front_kernel(
    omega_hbm,
    grads_hbm,
    summed_ref,
    basis_ref,
    panel_ref,
    blocks_ref,
    w,
    inv,
    omega_ref,
    grads,
    omegas,
    relay_in,
    joint,
    near_in,
    partial,
    part,
    rs_buf,
    mine,
    core_buf,
    chip,
    x_buf,
    x_sum,
    z_buf,
    strip,
    y_buf,
    sems,
    local_sems,
):
    spot = place()
    y, x, z, c = spot
    twin = along("c", spot, 1)
    near_y = [along("y", spot, k) for k in range(1, NY)]
    near_x = [along("x", spot, k) for k in range(1, NX)]
    near_z = [along("z", spot, k) for k in range(1, NZ)]
    loads = [pltpu.make_async_copy(omega_hbm, omega_ref, local_sems.at[NY])]
    loads[0].start()
    for k in (0, 1, 3, 2):
        columns = span(((y + k) % NY) * OWN, OWN)
        load = pltpu.make_async_copy(grads_hbm.at[:, :, columns], grads.at[k], local_sems.at[k])
        load.start()
        loads.append(load)
    greet([twin] + near_y + near_x + near_z)
    done, sent = [], []
    count = [0]

    def go(src, dst, peer):
        copy = ship(src, dst, sems.at[0, count[0]], sems.at[1, count[0]], peer)
        count[0] += 1
        done.append(copy)
        return copy

    def landed(copies):
        for copy in copies:
            copy.wait_recv()

    relays, nears = [None] * 2, [None] * 2

    SUB = ROWS // 2

    def columns(part_of, k):
        return span(((y + k) % NY) * OWN + (1 - part_of) * HALF, HALF)

    def launch(part_of):
        relays[part_of] = [
            [
                go(
                    grads_hbm.at[n, pl.ds(r * SUB, SUB), columns(part_of, 2)],
                    relay_in.at[part_of, n, pl.ds(r * SUB, SUB), :],
                    near_y[2 * n],
                )
                for n in range(2)
            ]
            for r in range(2)
        ]

    def launch_near(part_of):
        for copies in relays[part_of]:
            for copy in copies:
                copy.wait_send()
                sent.append(id(copy))
        nears[part_of] = [
            go(grads_hbm.at[1, :, columns(part_of, 1)], near_in.at[part_of, 0, 1], near_y[0]),
            go(grads_hbm.at[0, :, columns(part_of, 3)], near_in.at[part_of, 1, 0], near_y[2]),
        ]

    def in_rows(first_row, count_rows, work):
        def body(t, carry):
            work(pl.ds(pl.multiple_of(first_row + t * 32, 32), 32))
            return carry

        lax.fori_loop(0, count_rows // 32, body, 0)

    def combine(part_of):
        off = (1 - part_of) * HALF
        for r in range(2):
            for n, k in ((0, 1), (1, 3)):
                relays[part_of][r][n].wait_recv()

                def work(at):
                    own_term = grads[k, n, at, off : off + HALF].astype(F32)
                    joint[part_of, n, at, :] = (own_term + relay_in[part_of, n, at, :].astype(F32)).astype(BF)

                in_rows(r * SUB, SUB, work)
                at = pl.ds(r * SUB, SUB)
                nears[part_of].append(go(joint.at[part_of, n, at, :], near_in.at[part_of, n, n, at, :], near_y[k - 1]))

    def finish_sum(part_of):
        off = (1 - part_of) * HALF
        landed(nears[part_of])

        def work(at):
            for n in range(LAYERS):
                out = grads[0, n, at, off : off + HALF].astype(F32) + near_in[part_of, 0, n, at, :].astype(F32)
                summed_ref[n, at, off : off + HALF] = (out + near_in[part_of, 1, n, at, :].astype(F32)).astype(BF)

        in_rows(0, ROWS, work)

    strip_at = span(x * 256 + c * B + z * 16, 16)
    slices = [go(omega_hbm.at[strip_at, :], omegas.at[FAR - k, strip_at, :], near_y[k - 1]) for k in range(1, NY)]
    launch(0)

    def block(s, which, start, size):
        return omegas.at[s, pl.ds(pl.multiple_of(which * 256 + c * B + start, size), size), :]

    flights = []
    for s in range(FAR):
        slices[FAR - 1 - s].wait_recv()
        piece = omegas.at[s, strip_at, :]
        flights.append([go(piece, piece, peer) for peer in near_z])
    for load in loads:
        load.wait()
    for n in range(LAYERS):
        partial[n] = jnp.dot(grads[0, n, :, :HALF], omega_ref[:HALF, :], preferred_element_type=F32)
    launch_near(0)
    up, down = near_x[0], near_x[2]
    above, below, across = (x + 1) % NX, (x + NX - 1) % NX, (x + 2) % NX
    h = B // 2
    firsts, crossed, seconds = [], [], []
    for s in range(FAR):
        landed(flights[s])
        low, high, whole = block(s, x, 0, h), block(s, x, h, h), block(s, x, 0, B)
        firsts.append([go(low, low, up), go(high, high, down), go(high, high, up), go(low, low, down)])
        crossed.append([go(whole, whole, twin)])
    combine(0)
    for s in range(FAR):
        firsts[s][0].wait_recv()
        low = block(s, below, 0, h)
        seconds.append([go(low, low, up)])
        firsts[s][1].wait_recv()
        high = block(s, above, h, h)
        seconds[s].append(go(high, high, down))
        landed(firsts[s][2:])
        for which in (below, above):
            whole = block(s, which, 0, B)
            crossed[s].append(go(whole, whole, twin))
    for s in range(FAR):
        landed(seconds[s])
        whole = block(s, across, 0, B)
        crossed[s].append(go(whole, whole, twin))
    for s in range(FAR):
        landed(crossed[s])
        for n in range(LAYERS):
            partial[n] += jnp.dot(grads[s + 1, n, :, :HALF], omegas[s], preferred_element_type=F32)
    finish_sum(0)
    for n in range(LAYERS):
        out = partial[n] + jnp.dot(summed_ref[n, :, HALF:], omega_ref[HALF:, :], preferred_element_type=F32)
        part[n] = out.astype(BF)

    q = ROWS // NY
    own = span(y * q, q)
    first = [
        [
            go(part.at[n, span(((y + k) % NY) * q, q), :], rs_buf.at[k - 1, n], near_y[k - 1])
            for k in range(1, NY)
        ]
        for n in range(LAYERS)
    ]
    spread = []
    for n in range(LAYERS):
        landed(first[n])
        if n == 1:
            launch(1)
        total = part[n, own, :].astype(F32)
        for k in range(1, NY):
            total = total + rs_buf[k - 1, n].astype(F32)
        panel_ref[n, own, :] = total.astype(BF)
        whole = panel_ref[n, own, :]
        row = n * 10 * B
        for i in range(4):
            wide = (i + 1) * B
            out = lax.dot_general(whole[:, i * B : wide], whole[:, :wide], TN, preferred_element_type=F32)
            for j in range(i + 1):
                mine[row : row + B, :] = out[:, j * B : j * B + B]
                row += B
        if n == 0:
            start, size = STREAMS[0]
            half = size // 2
            flight = [
                [go(mine.at[rows_at(start + (1 - c) * half, half), :], core_buf.at[pl.ds(start // 2, half), :], twin)]
            ]
    start, size = STREAMS[1]
    half = size // 2
    flight.append(
        [go(mine.at[rows_at(start + (1 - c) * half, half), :], core_buf.at[pl.ds(start // 2, half), :], twin)]
    )

    for s, (start, size) in enumerate(STREAMS):
        half, quarter = size // 2, size // 8
        landed(flight[s])
        here = pl.ds(start // 2, half)
        chip[here, :] = mine[rows_at(start + c * half, half), :] + core_buf[here, :]
        flight[s] = [
            go(
                chip.at[rows_at(start // 2 + ((x + k) % NX) * quarter, quarter), :],
                x_buf.at[k - 1, pl.ds(start // 8, quarter), :],
                near_x[k - 1],
            )
            for k in range(1, NX)
        ]
    for s, (start, size) in enumerate(STREAMS):
        quarter, piece = size // 8, size // 64
        landed(flight[s])
        total = chip[rows_at(start // 2 + x * quarter, quarter), :]
        for k in range(1, NX):
            total = total + x_buf[k - 1, start // 8 : start // 8 + quarter, :]
        x_sum[start // 8 : start // 8 + quarter, :] = total
        flight[s] = [
            go(
                x_sum.at[rows_at(start // 8 + ((z + k) % NZ) * piece, piece), :],
                z_buf.at[k - 1, pl.ds(start // 64, piece), :],
                near_z[k - 1],
            )
            for k in range(1, NZ)
        ]
    for s, (start, size) in enumerate(STREAMS):
        piece = size // 64
        landed(flight[s])
        here = pl.ds(start // 64, piece)
        total = x_sum[rows_at(start // 8 + z * piece, piece), :]
        for k in range(1, NZ):
            total = total + z_buf[k - 1, here, :]
        strip[here, :] = total
        flight[s] = [go(strip.at[here, :], y_buf.at[k - 1, here, :], near_y[k - 1]) for k in range(1, NY)]
    for s, (start, size) in enumerate(STREAMS):
        half, quarter, piece = size // 2, size // 8, size // 64
        landed(flight[s])
        here = pl.ds(start // 64, piece)
        total = strip[here, :]
        for k in range(1, NY):
            total = total + y_buf[k - 1, here, :]
        at = rows_at(start + c * half + x * quarter + z * piece, piece)
        blocks_ref[at, :] = total
        flight[s] = [go(blocks_ref.at[at, :], blocks_ref.at[at, :], peer) for peer in near_z]
    for k in range(1, NY):
        spread.append(go(panel_ref.at[:, own, :], panel_ref.at[:, own, :], near_y[k - 1]))
    launch_near(1)
    combine(1)
    for s, (start, size) in enumerate(STREAMS):
        half, quarter = size // 2, size // 8
        landed(flight[s])
        at = rows_at(start + c * half + x * quarter, quarter)
        flight[s] = [go(blocks_ref.at[at, :], blocks_ref.at[at, :], peer) for peer in near_x]
    for s, (start, size) in enumerate(STREAMS):
        half = size // 2
        landed(flight[s])
        at = rows_at(start + c * half, half)
        flight[s] = [go(blocks_ref.at[at, :], blocks_ref.at[at, :], twin)]
    for copies in flight:
        landed(copies)
    for n in range(LAYERS):
        row = n * 10 * B
        for i in range(4):
            for j in range(i + 1):
                block = blocks_ref[row : row + B, :]
                row += B
                w[n, i * B : i * B + B, j * B : j * B + B] = block
                if i != j:
                    w[n, j * B : j * B + B, i * B : i * B + B] = block.T

    def step(k, carry):
        here = span(k * B, B)
        inv[...] = eliminate(w[:, here, here])
        for at in range(4):

            @pl.when(k == at)
            def _():
                a, z = at * B, at * B + B
                for n in range(LAYERS):
                    inverse = inv[n]
                    right = jnp.dot(inverse, w[n, a:z, :], precision=HIGHEST, preferred_element_type=F32)
                    pieces = [right[:, :a], inverse, right[:, z:]]
                    right = jnp.concatenate([p for p in pieces if p.shape[1]], axis=1)
                    if z < RANK:
                        left = lax.dot_general(
                            w[n, z:, a:z], inverse, NT, precision=HIGHEST, preferred_element_type=F32
                        )
                        w[n, z:, a:z] = jnp.zeros((RANK - z, B), F32)
                        w[n, z:, :] = w[n, z:, :] - jnp.dot(
                            left, right, precision=HIGHEST, preferred_element_type=F32
                        )
                        right = jnp.concatenate([right[:, :z], jnp.zeros((B, RANK - z), F32)], axis=1)
                    w[n, a:z, :] = right

        return carry

    lax.fori_loop(0, 4, step, 0)
    landed(spread)
    for n in range(LAYERS):
        rest = w[n]
        basis = jnp.zeros((ROWS, RANK), F32)
        for _ in range(3):
            part = rest.astype(BF)
            rest = rest - part.astype(F32)
            basis = basis + lax.dot_general(panel_ref[n], part, NT, preferred_element_type=F32)
        basis_ref[n] = basis.astype(BF)
    finish_sum(1)
    for copy in done:
        if id(copy) not in sent:
            copy.wait_send()


def front(omega, grads):
    vmem = pl.BlockSpec(memory_space=pltpu.VMEM)
    return pl.pallas_call(
        front_kernel,
        out_shape=(
            jax.ShapeDtypeStruct((LAYERS, ROWS, OWN), BF),
            jax.ShapeDtypeStruct((LAYERS, ROWS, RANK), BF),
        ),
        in_specs=[pl.BlockSpec(memory_space=pltpu.HBM)] * 2,
        out_specs=(vmem, vmem),
        scratch_shapes=[
            pltpu.VMEM((LAYERS, ROWS, RANK), BF),
            pltpu.VMEM((BLOCKS, B), F32),
            pltpu.VMEM((LAYERS, RANK, RANK), F32),
            pltpu.VMEM((LAYERS, B, B), F32),
            pltpu.VMEM((OWN, RANK), BF),
            pltpu.VMEM((NY, LAYERS, ROWS, OWN), BF),
            pltpu.VMEM((FAR, HALF, RANK), BF),
            pltpu.VMEM((2, LAYERS, ROWS, HALF), BF),
            pltpu.VMEM((2, LAYERS, ROWS, HALF), BF),
            pltpu.VMEM((2, 2, LAYERS, ROWS, HALF), BF),
            pltpu.VMEM((LAYERS, ROWS, RANK), F32),
            pltpu.VMEM((LAYERS, ROWS, RANK), BF),
            pltpu.VMEM((NY - 1, LAYERS, ROWS // NY, RANK), BF),
            pltpu.VMEM((BLOCKS, B), F32),
            pltpu.VMEM((BLOCKS // 2, B), F32),
            pltpu.VMEM((BLOCKS // 2, B), F32),
            pltpu.VMEM((NX - 1, BLOCKS // 8, B), F32),
            pltpu.VMEM((BLOCKS // 8, B), F32),
            pltpu.VMEM((NZ - 1, BLOCKS // 64, B), F32),
            pltpu.VMEM((BLOCKS // 64, B), F32),
            pltpu.VMEM((NY - 1, BLOCKS // 64, B), F32),
            pltpu.SemaphoreType.DMA((2, 160)),
            pltpu.SemaphoreType.DMA((NY + 1,)),
        ],
        compiler_params=pltpu.CompilerParams(collective_id=0, has_side_effects=True, vmem_limit_bytes=50 << 20),
    )(omega, grads)


RUNS = ((0, 0), (1, 0), (0, 512), (1, 512))
WIDE = 512


def tail_kernel(
    basis_ref,
    summed_ref,
    first_ref,
    second_ref,
    new_first_ref,
    new_second_ref,
    delta_ref,
    summed,
    twin_basis,
    twin_summed,
    twin_first,
    twin_second,
    back_first,
    back_second,
    relay_out,
    relay_in,
    near_out,
    near_in,
    x_own,
    z_out,
    z_in,
    z_own,
    joined,
    gathered,
    sems,
    local_sems,
):
    spot = place()
    y, x, z, c = spot
    twin = along("c", spot, 1)
    up, down = along("x", spot, 1), along("x", spot, NX - 1)
    near_z = [along("z", spot, k) for k in range(1, NZ)]
    mine, other = span(c * HALF, HALF), span((1 - c) * HALF, HALF)
    runs = range(len(RUNS))

    def cut(core, r):
        return pl.ds(pl.multiple_of(core * HALF + RUNS[r][1], WIDE), WIDE)

    loads = []
    for r in runs:
        load = pltpu.make_async_copy(summed_ref.at[RUNS[r][0], :, cut(c, r)], summed.at[r], local_sems.at[r])
        load.start()
        loads.append(load)
    greet([twin, up, down] + near_z)
    done = []
    count = [0]

    def go(src, dst, peer):
        copy = ship(src, dst, sems.at[0, count[0]], sems.at[1, count[0]], peer)
        count[0] += 1
        done.append(copy)
        return copy

    def landed(copies):
        for copy in copies:
            copy.wait_recv()

    got = []
    for r in runs:
        copies = [go(summed_ref.at[RUNS[r][0], :, cut(1 - c, r)], twin_summed.at[r], twin)]
        if r < LAYERS:
            copies.append(go(basis_ref.at[r], twin_basis.at[r], twin))
        got.append(copies)
    moments = [
        go(first_ref.at[:, :, other], twin_first, twin),
        go(second_ref.at[:, :, other], twin_second, twin),
    ]

    def product(r, start, size):
        here, n = span(start, size), RUNS[r][0]
        out = lax.dot_general(basis_ref[n, :, here], summed[r], TN, preferred_element_type=F32)
        return out + lax.dot_general(twin_basis[n, :, here], twin_summed[r], TN, preferred_element_type=F32)

    h = B // 2
    above, below, across = ((x + 1) % NX) * B, ((x + NX - 1) % NX) * B, ((x + 2) % NX) * B
    relays, nears, spreads, firsts, seconds = {}, {}, {}, {}, {}
    z_copies, crossed = {}, {}
    slot = span(x * B + z * 16, 16)
    ours, theirs = span(c * 8, 8), span((1 - c) * 8, 8)

    def part(n, start, size):
        return gathered.at[c, n, pl.ds(pl.multiple_of(start, size), size), :]

    def multiply(n):
        landed(got[n])
        loads[n].wait()
        far = product(n, across, B)
        relay_out[n, 0] = far[:h].astype(BF)
        relay_out[n, 1] = far[h:].astype(BF)
        relays[n] = [go(relay_out.at[n, 0], relay_in.at[n, 0], up), go(relay_out.at[n, 1], relay_in.at[n, 1], down)]
        x_own[n, 1] = product(n, above, B)
        near_out[n, 0, h:, :] = x_own[n, 1, h:, :].astype(BF)
        nears[n] = [go(near_out.at[n, 0, pl.ds(h, h), :], near_in.at[n, 0, pl.ds(h, h), :], up)]
        x_own[n, 2] = product(n, below, B)
        near_out[n, 1, :h, :] = x_own[n, 2, :h, :].astype(BF)
        nears[n].append(go(near_out.at[n, 1, pl.ds(0, h), :], near_in.at[n, 1, pl.ds(0, h), :], down))
        x_own[n, 0] = product(n, x * B, B)

    def pass_on(n):
        relays[n][0].wait_recv()
        near_out[n, 0, :h, :] = (x_own[n, 1, :h, :] + relay_in[n, 0].astype(F32)).astype(BF)
        nears[n].append(go(near_out.at[n, 0, pl.ds(0, h), :], near_in.at[n, 0, pl.ds(0, h), :], up))
        relays[n][1].wait_recv()
        near_out[n, 1, h:, :] = (x_own[n, 2, h:, :] + relay_in[n, 1].astype(F32)).astype(BF)
        nears[n].append(go(near_out.at[n, 1, pl.ds(h, h), :], near_in.at[n, 1, pl.ds(h, h), :], down))

    def over_z(n):
        landed(nears[n])
        total = x_own[n, 0] + near_in[n, 0].astype(F32) + near_in[n, 1].astype(F32)
        x_own[n, 0] = total
        z_out[n] = total.astype(BF)
        z_copies[n] = [
            go(z_out.at[n, span(((z + k) % NZ) * 16, 16), :], z_in.at[n, k - 1], near_z[k - 1]) for k in range(1, NZ)
        ]

    def adam(projected, first, second):
        new_first = 0.9 * first + 0.1 * projected
        new_second = 0.999 * second + 0.001 * projected * projected
        return new_first, new_second, new_first / (jnp.sqrt(new_second) + 1e-08)

    def update(n):
        layer, off = RUNS[n]
        here, there = cut(c, n), pl.ds(off, WIDE)
        if n == 0:
            landed(moments)
        landed(z_copies[n])
        total = x_own[n, 0, span(z * 16, 16), :]
        for k in range(1, NZ):
            total = total + z_in[n, k - 1].astype(F32)
        z_own[n] = total
        new_first, new_second, fresh = adam(z_own[n, ours, :], first_ref[:, layer, here], second_ref[:, layer, here])
        new_first_ref[:, layer, here] = new_first
        new_second_ref[:, layer, here] = new_second
        joined[n, ours, :] = fresh
        new_first, new_second, fresh = adam(z_own[n, theirs, :], twin_first[:, layer, there], twin_second[:, layer, there])
        back_first[:, layer, there] = new_first
        back_second[:, layer, there] = new_second
        joined[n, theirs, :] = fresh
        gathered[c, n, slot, :] = joined[n].astype(BF)
        piece = gathered.at[c, n, slot, :]
        spreads[n] = [go(piece, piece, peer) for peer in near_z]

    def over_x(n):
        landed(spreads[n])
        low, high, whole = part(n, x * B, h), part(n, x * B + h, h), part(n, x * B, B)
        firsts[n] = [go(low, low, up), go(high, high, down), go(high, high, up), go(low, low, down)]
        crossed[n] = [go(whole, whole, twin)]

    def forward(n):
        firsts[n][0].wait_recv()
        low = part(n, below, h)
        seconds[n] = [go(low, low, up)]
        firsts[n][1].wait_recv()
        high = part(n, above + h, h)
        seconds[n].append(go(high, high, down))
        landed(firsts[n][2:])
        for start in (below, above):
            whole = part(n, start, B)
            crossed[n].append(go(whole, whole, twin))

    def cross(n):
        landed(seconds[n])
        whole = part(n, across, B)
        crossed[n].append(go(whole, whole, twin))

    def apply(n):
        layer, off = RUNS[n]
        landed(crossed[n])
        for core in range(NC):
            out = jnp.dot(basis_ref[layer], gathered[core, n], preferred_element_type=F32)
            delta_ref[layer, :, core * HALF + off : core * HALF + off + WIDE] = out.astype(BF)

    stages = (multiply, pass_on, over_z, update, over_x, forward, cross, apply)
    for tick in range(len(RUNS) + len(stages) - 1):
        for lag, stage in enumerate(stages):
            if 0 <= tick - lag < len(RUNS):
                stage(tick - lag)
    backs = [
        go(back_first, new_first_ref.at[:, :, mine], twin),
        go(back_second, new_second_ref.at[:, :, mine], twin),
    ]
    landed(backs)
    for copy in done:
        copy.wait_send()


def tail(basis, summed, first, second):
    vmem = pl.BlockSpec(memory_space=pltpu.VMEM)
    return pl.pallas_call(
        tail_kernel,
        out_shape=(
            jax.ShapeDtypeStruct((8, LAYERS, OWN), F32),
            jax.ShapeDtypeStruct((8, LAYERS, OWN), F32),
            jax.ShapeDtypeStruct((LAYERS, ROWS, OWN), BF),
        ),
        in_specs=[vmem, pl.BlockSpec(memory_space=pl.ANY), vmem, vmem],
        out_specs=(vmem,) * 3,
        scratch_shapes=[
            pltpu.VMEM((4, ROWS, WIDE), BF),
            pltpu.VMEM((LAYERS, ROWS, RANK), BF),
            pltpu.VMEM((4, ROWS, WIDE), BF),
            pltpu.VMEM((8, LAYERS, HALF), F32),
            pltpu.VMEM((8, LAYERS, HALF), F32),
            pltpu.VMEM((8, LAYERS, HALF), F32),
            pltpu.VMEM((8, LAYERS, HALF), F32),
            pltpu.VMEM((4, 2, B // 2, WIDE), BF),
            pltpu.VMEM((4, 2, B // 2, WIDE), BF),
            pltpu.VMEM((4, 2, B, WIDE), BF),
            pltpu.VMEM((4, 2, B, WIDE), BF),
            pltpu.VMEM((4, 3, B, WIDE), F32),
            pltpu.VMEM((4, B, WIDE), BF),
            pltpu.VMEM((4, NZ - 1, 16, WIDE), BF),
            pltpu.VMEM((4, 16, WIDE), F32),
            pltpu.VMEM((4, 16, WIDE), F32),
            pltpu.VMEM((NC, 4, RANK, WIDE), BF),
            pltpu.SemaphoreType.DMA((2, 144)),
            pltpu.SemaphoreType.DMA((4,)),
        ],
        compiler_params=pltpu.CompilerParams(collective_id=1, has_side_effects=True, vmem_limit_bytes=48 << 20),
    )(basis, summed, first, second)


def local(grad_parts, omega, first_moment, second_moment):
    summed, basis = front(omega, grad_parts[0])
    return tail(basis, summed, first_moment, second_moment)


def solution(mesh):
    return jax.shard_map(
        local,
        mesh=mesh,
        in_specs=(P("dp", None, "mp", None), P("dp", None), P("mp", None, "dp"), P("mp", None, "dp")),
        out_specs=(P("mp", None, "dp"), P("mp", None, "dp"), P(None, "mp", "dp")),
        check_vma=False,
    )
```

```python
import functools

import jax
import jax.numpy as jnp
from jax import lax
from jax.experimental import pallas as pl
from jax.experimental.pallas import tpu as pltpu
from jax.sharding import PartitionSpec as P

HIGHEST = lax.Precision.HIGHEST
MESH = pl.DeviceIdType.MESH
NT = (((1,), (1,)), ((), ()))
TN = (((0,), (0,)), ((), ()))
BF = jnp.bfloat16
F32 = jnp.float32

LAYERS = 2
ROWS = 256
D = 8192
OWN = 2048
HALF = 1024
RANK = 512
B = 128
NY, NX, NZ, NC = 4, 4, 8, 2


def place():
    mp = lax.axis_index("mp")
    return lax.axis_index("dp"), mp // (NZ * NC), (mp // NC) % NZ, mp % NC


def device(y, x, z, c):
    return {"dp": y, "mp": x * (NZ * NC) + z * NC + c}


def greet(peers):
    barrier = pltpu.get_barrier_semaphore()
    for peer in peers:
        pl.semaphore_signal(barrier, inc=1, device_id=peer, device_id_type=MESH)
    pl.semaphore_wait(barrier, len(peers))


def along(axis, spot, k):
    y, x, z, c = spot
    if axis == "y":
        return device((y + k) % NY, x, z, c)
    if axis == "x":
        return device(y, (x + k) % NX, z, c)
    if axis == "z":
        return device(y, x, (z + k) % NZ, c)
    return device(y, x, z, 1 - c)


def ship(src, dst, send, recv, peer):
    copy = pltpu.make_async_remote_copy(
        src_ref=src, dst_ref=dst, send_sem=send, recv_sem=recv, device_id=peer, device_id_type=MESH
    )
    copy.start()
    return copy


def span(start, size):
    return pl.ds(pl.multiple_of(start, size), size)


RUNS = ((0, 0), (1, 0), (0, 512), (1, 512))
WIDE = 512


def cut(core, r):
    return pl.ds(pl.multiple_of(core * HALF + RUNS[r][1], WIDE), WIDE)


def finish(spot, go, landed, moments, got, refs, held, scratch):
    y, x, z, c = spot
    first_ref, second_ref, new_first_ref, new_second_ref, delta_ref = refs
    summed_ref, basis_ref, x_own = held
    (
        twin_basis,
        twin_summed,
        twin_first,
        twin_second,
        back_first,
        back_second,
        relay_out,
        relay_in,
        near_out,
        near_in,
        z_out,
        z_in,
        z_own,
        joined,
        gathered,
    ) = scratch
    twin = along("c", spot, 1)
    up, down = along("x", spot, 1), along("x", spot, NX - 1)
    near_z = [along("z", spot, k) for k in range(1, NZ)]
    mine = span(c * HALF, HALF)

    def product(r, start, size):
        here, n = span(start, size), RUNS[r][0]
        out = lax.dot_general(basis_ref[n, :, here], summed_ref[n, :, cut(c, r)], TN, preferred_element_type=F32)
        return out + lax.dot_general(twin_basis[n, :, here], twin_summed[r], TN, preferred_element_type=F32)

    h = B // 2
    above, below, across = ((x + 1) % NX) * B, ((x + NX - 1) % NX) * B, ((x + 2) % NX) * B
    relays, nears, spreads, firsts, seconds = {}, {}, {}, {}, {}
    z_copies, crossed = {}, {}
    slot = span(x * B + z * 16, 16)
    ours, theirs = span(c * 8, 8), span((1 - c) * 8, 8)

    def part(n, start, size):
        return gathered.at[c, n, pl.ds(pl.multiple_of(start, size), size), :]

    def kept(n, start, size):
        return slice((n % 2) * 2 * B + start, (n % 2) * 2 * B + start + size)

    def multiply(n):
        landed(got[n])
        far = product(n, across, B)
        relay_out[n, 0] = far[:h].astype(BF)
        relay_out[n, 1] = far[h:].astype(BF)
        relays[n] = [go(relay_out.at[n, 0], relay_in.at[n, 0], up), go(relay_out.at[n, 1], relay_in.at[n, 1], down)]
        out = product(n, above, B)
        x_own[n // 2, kept(n, B, h), :] = out[:h]
        near_out[n, 0, h:, :] = out[h:].astype(BF)
        nears[n] = [go(near_out.at[n, 0, pl.ds(h, h), :], near_in.at[n, 0, pl.ds(h, h), :], up)]
        out = product(n, below, B)
        x_own[n // 2, kept(n, B + h, h), :] = out[h:]
        near_out[n, 1, :h, :] = out[:h].astype(BF)
        nears[n].append(go(near_out.at[n, 1, pl.ds(0, h), :], near_in.at[n, 1, pl.ds(0, h), :], down))
        x_own[n // 2, kept(n, 0, B), :] = product(n, x * B, B)

    def pass_on(n):
        relays[n][0].wait_recv()
        near_out[n, 0, :h, :] = (x_own[n // 2, kept(n, B, h), :] + relay_in[n, 0].astype(F32)).astype(BF)
        nears[n].append(go(near_out.at[n, 0, pl.ds(0, h), :], near_in.at[n, 0, pl.ds(0, h), :], up))
        relays[n][1].wait_recv()
        near_out[n, 1, h:, :] = (x_own[n // 2, kept(n, B + h, h), :] + relay_in[n, 1].astype(F32)).astype(BF)
        nears[n].append(go(near_out.at[n, 1, pl.ds(h, h), :], near_in.at[n, 1, pl.ds(h, h), :], down))

    def over_z(n):
        landed(nears[n])
        total = x_own[n // 2, kept(n, 0, B), :] + near_in[n, 0].astype(F32) + near_in[n, 1].astype(F32)
        x_own[n // 2, kept(n, 0, B), :] = total
        z_out[n] = total.astype(BF)
        z_copies[n] = [
            go(z_out.at[n, span(((z + k) % NZ) * 16, 16), :], z_in.at[n, k - 1], near_z[k - 1]) for k in range(1, NZ)
        ]

    def adam(projected, first, second):
        new_first = 0.9 * first + 0.1 * projected
        new_second = 0.999 * second + 0.001 * projected * projected
        return new_first, new_second, new_first / (jnp.sqrt(new_second) + 1e-08)

    def update(n):
        layer, off = RUNS[n]
        here, there = cut(c, n), pl.ds(off, WIDE)
        if n == 0:
            landed(moments)
        landed(z_copies[n])
        total = x_own[n // 2, pl.ds(pl.multiple_of((n % 2) * 2 * B + z * 16, 16), 16), :]
        for k in range(1, NZ):
            total = total + z_in[n, k - 1].astype(F32)
        z_own[n] = total
        new_first, new_second, fresh = adam(z_own[n, ours, :], first_ref[:, layer, here], second_ref[:, layer, here])
        new_first_ref[:, layer, here] = new_first
        new_second_ref[:, layer, here] = new_second
        joined[n, ours, :] = fresh
        new_first, new_second, fresh = adam(z_own[n, theirs, :], twin_first[:, layer, there], twin_second[:, layer, there])
        back_first[:, layer, there] = new_first
        back_second[:, layer, there] = new_second
        joined[n, theirs, :] = fresh
        gathered[c, n, slot, :] = joined[n].astype(BF)
        piece = gathered.at[c, n, slot, :]
        spreads[n] = [go(piece, piece, peer) for peer in near_z]

    def over_x(n):
        landed(spreads[n])
        low, high, whole = part(n, x * B, h), part(n, x * B + h, h), part(n, x * B, B)
        firsts[n] = [go(low, low, up), go(high, high, down), go(high, high, up), go(low, low, down)]
        crossed[n] = [go(whole, whole, twin)]

    def forward(n):
        firsts[n][0].wait_recv()
        low = part(n, below, h)
        seconds[n] = [go(low, low, up)]
        firsts[n][1].wait_recv()
        high = part(n, above + h, h)
        seconds[n].append(go(high, high, down))
        landed(firsts[n][2:])
        for start in (below, above):
            whole = part(n, start, B)
            crossed[n].append(go(whole, whole, twin))

    def cross(n):
        landed(seconds[n])
        whole = part(n, across, B)
        crossed[n].append(go(whole, whole, twin))

    def apply(n):
        layer, off = RUNS[n]
        landed(crossed[n])
        for core in range(NC):
            out = jnp.dot(basis_ref[layer], gathered[core, n], preferred_element_type=F32)
            delta_ref[layer, :, core * HALF + off : core * HALF + off + WIDE] = out.astype(BF)

    stages = (multiply, pass_on, over_z, update, over_x, forward, cross, apply)
    for tick in range(len(RUNS) + len(stages) - 1):
        for lag, stage in enumerate(stages):
            if 0 <= tick - lag < len(RUNS):
                stage(tick - lag)
    backs = [
        go(back_first, new_first_ref.at[:, :, mine], twin),
        go(back_second, new_second_ref.at[:, :, mine], twin),
    ]
    landed(backs)


def eliminate(whole):
    lane = lax.broadcasted_iota(jnp.int32, (1, 8, B), 2)
    sub = lax.broadcasted_iota(jnp.int32, (1, 8, B), 1)
    sub4 = lax.broadcasted_iota(jnp.int32, (1, 1, 8, B), 2)
    found = []
    for b in range(B // 8):
        inside = (lane >= 8 * b) & (lane < 8 * b + 8)
        top = whole[:, :8, :]
        cols = [top[:, :, 8 * b + k : 8 * b + k + 1] for k in range(8)]
        cols = jnp.stack([jnp.broadcast_to(col, (LAYERS, 8, B)) for col in cols], axis=1)
        start = jnp.where(inside, (lane == sub + 8 * b).astype(F32), top)
        state = jnp.concatenate([cols, start[:, None]], axis=1)
        forward = start
        scale = jnp.zeros((LAYERS, 8, B), F32)
        for k in range(8):
            column = state[:, k]
            pivot = column[:, k : k + 1, :]
            inverse = 1.0 / pivot
            factor = column * inverse
            line = state[:, :, k : k + 1, :]
            state = jnp.where(sub4 == k, line * inverse[:, None], state - factor[:, None] * line)
            forward = jnp.where(sub > k, forward - factor * forward[:, k : k + 1, :], forward)
            scale = jnp.where(sub == k, pivot, scale)
        found.append(jnp.where(lane < 8 * b + 8, forward, 0.0) * lax.rsqrt(scale))
        if b < B // 8 - 1:
            rest = whole[:, 8:, :]
            total = None
            for k in range(8):
                term = rest[:, :, 8 * b + k : 8 * b + k + 1] * state[:, 8, k : k + 1, :]
                total = term if total is None else total + term
            whole = jnp.where(inside[:, :1], 0.0, rest) - total
    return jnp.concatenate(found, axis=1)


STREAMS = ((0, 1024), (1024, 1536))
BLOCKS = LAYERS * 10 * B
FAR = NY - 1
SPLIT, EXTRA = 1024, 256
KEPT = SPLIT + EXTRA
PARTS = ((KEPT, OWN - KEPT), (0, KEPT))


def rows_at(start, size):
    return pl.ds(pl.multiple_of(start, 8), size)


def refresh_kernel(
    omega_hbm,
    grads_hbm,
    first_ref,
    second_ref,
    new_first_ref,
    new_second_ref,
    delta_ref,
    summed_ref,
    basis_ref,
    panel_ref,
    blocks_ref,
    w,
    inv,
    omega_ref,
    grads,
    omegas,
    relay_a,
    relay_b,
    joint_a,
    joint_b,
    near_a,
    near_b,
    partial,
    part,
    rs_buf,
    mine,
    core_buf,
    chip,
    x_buf,
    x_sum,
    z_buf,
    strip,
    y_buf,
    sems,
    local_sems,
    *tail_scratch,
):
    spot = place()
    y, x, z, c = spot
    twin = along("c", spot, 1)
    near_y = [along("y", spot, k) for k in range(1, NY)]
    near_x = [along("x", spot, k) for k in range(1, NX)]
    near_z = [along("z", spot, k) for k in range(1, NZ)]
    loads = [pltpu.make_async_copy(omega_hbm, omega_ref, local_sems.at[NY])]
    loads[0].start()
    for k in (0, 1, 3, 2):
        columns = span(((y + k) % NY) * OWN, OWN)
        load = pltpu.make_async_copy(grads_hbm.at[:, :, columns], grads.at[k], local_sems.at[k])
        load.start()
        loads.append(load)
    greet([twin] + near_y + near_x + near_z)
    done, sent = [], []
    count = [0]

    def go(src, dst, peer):
        copy = ship(src, dst, sems.at[0, count[0]], sems.at[1, count[0]], peer)
        count[0] += 1
        done.append(copy)
        return copy

    def landed(copies):
        for copy in copies:
            copy.wait_recv()

    twin_basis, twin_summed, twin_first, twin_second = tail_scratch[:4]
    other = span((1 - c) * HALF, HALF)
    relay_in, joint, near_in = (relay_a, relay_b), (joint_a, joint_b), (near_a, near_b)
    relays, nears = [None] * 2, [None] * 2

    SUB = ROWS // 2

    def columns(part_of, k):
        off, width = PARTS[part_of]
        return pl.ds(pl.multiple_of(((y + k) % NY) * OWN + off, 2 * B), width)

    def launch(part_of):
        relays[part_of] = [
            [
                go(
                    grads_hbm.at[n, pl.ds(r * SUB, SUB), columns(part_of, 2)],
                    relay_in[part_of].at[n, pl.ds(r * SUB, SUB), :],
                    near_y[2 * n],
                )
                for n in range(2)
            ]
            for r in range(2)
        ]

    def launch_near(part_of):
        for copies in relays[part_of]:
            for copy in copies:
                copy.wait_send()
                sent.append(id(copy))
        nears[part_of] = [
            go(grads_hbm.at[1, :, columns(part_of, 1)], near_in[part_of].at[0, 1], near_y[0]),
            go(grads_hbm.at[0, :, columns(part_of, 3)], near_in[part_of].at[1, 0], near_y[2]),
        ]

    def in_rows(first_row, count_rows, work):
        def body(t, carry):
            work(pl.ds(pl.multiple_of(first_row + t * 32, 32), 32))
            return carry

        lax.fori_loop(0, count_rows // 32, body, 0)

    def combine(part_of):
        off, width = PARTS[part_of]
        for r in range(2):
            for n, k in ((0, 1), (1, 3)):
                relays[part_of][r][n].wait_recv()

                def work(at):
                    own_term = grads[k, n, at, off : off + width].astype(F32)
                    joint[part_of][n, at, :] = (own_term + relay_in[part_of][n, at, :].astype(F32)).astype(BF)

                in_rows(r * SUB, SUB, work)
                at = pl.ds(r * SUB, SUB)
                nears[part_of].append(
                    go(joint[part_of].at[n, at, :], near_in[part_of].at[n, n, at, :], near_y[k - 1])
                )

    def finish_sum(part_of):
        off, width = PARTS[part_of]
        landed(nears[part_of])

        def work(at):
            for n in range(LAYERS):
                out = grads[0, n, at, off : off + width].astype(F32) + near_in[part_of][0, n, at, :].astype(F32)
                summed_ref[n, at, off : off + width] = (out + near_in[part_of][1, n, at, :].astype(F32)).astype(BF)

        in_rows(0, ROWS, work)

    strip_at = span(x * 256 + c * B + z * 16, 16)
    slices = [go(omega_hbm.at[strip_at, :], omegas.at[FAR - k, strip_at, :], near_y[k - 1]) for k in range(1, NY)]
    extra_at = rows_at(SPLIT + c * B + z * 16, 16)
    extras = [go(omega_hbm.at[extra_at, :], omegas.at[FAR - k, extra_at, :], near_y[k - 1]) for k in range(1, NY)]
    launch(0)
    moments = [
        go(first_ref.at[:, :, other], twin_first, twin),
        go(second_ref.at[:, :, other], twin_second, twin),
    ]

    def block(s, which, start, size):
        return omegas.at[s, pl.ds(pl.multiple_of(which * 256 + c * B + start, size), size), :]

    flights = []
    for s in range(FAR):
        slices[FAR - 1 - s].wait_recv()
        piece = omegas.at[s, strip_at, :]
        flights.append([go(piece, piece, peer) for peer in near_z])
    landed(extras)
    piece = omegas.at[:, extra_at, :]
    extras = [go(piece, piece, peer) for peer in near_z]
    for load in loads:
        load.wait()
    for n in range(LAYERS):
        partial[n] = jnp.dot(grads[0, n, :, :KEPT], omega_ref[:KEPT, :], preferred_element_type=F32)
    launch_near(0)
    up, down = near_x[0], near_x[2]
    above, below, across = (x + 1) % NX, (x + NX - 1) % NX, (x + 2) % NX
    h = B // 2
    firsts, crossed, seconds = [], [], []
    for s in range(FAR):
        landed(flights[s])
        low, high, whole = block(s, x, 0, h), block(s, x, h, h), block(s, x, 0, B)
        firsts.append([go(low, low, up), go(high, high, down), go(high, high, up), go(low, low, down)])
        crossed.append([go(whole, whole, twin)])
    combine(0)
    for s in range(FAR):
        firsts[s][0].wait_recv()
        low = block(s, below, 0, h)
        seconds.append([go(low, low, up)])
        firsts[s][1].wait_recv()
        high = block(s, above, h, h)
        seconds[s].append(go(high, high, down))
        landed(firsts[s][2:])
        for which in (below, above):
            whole = block(s, which, 0, B)
            crossed[s].append(go(whole, whole, twin))
    landed(extras)
    piece = omegas.at[:, rows_at(SPLIT + c * B, B), :]
    crossed[0].append(go(piece, piece, twin))
    for s in range(FAR):
        landed(seconds[s])
        whole = block(s, across, 0, B)
        crossed[s].append(go(whole, whole, twin))
    for s in range(FAR):
        landed(crossed[s])
        for n in range(LAYERS):
            partial[n] += jnp.dot(grads[s + 1, n, :, :KEPT], omegas[s], preferred_element_type=F32)
    finish_sum(0)
    for n in range(LAYERS):
        out = partial[n] + jnp.dot(summed_ref[n, :, KEPT:], omega_ref[KEPT:, :], preferred_element_type=F32)
        part[n] = out.astype(BF)

    q = ROWS // NY
    own = span(y * q, q)
    first = [
        [
            go(part.at[n, span(((y + k) % NY) * q, q), :], rs_buf.at[k - 1, n], near_y[k - 1])
            for k in range(1, NY)
        ]
        for n in range(LAYERS)
    ]
    spread = []
    for n in range(LAYERS):
        landed(first[n])
        if n == 1:
            launch(1)
        total = part[n, own, :].astype(F32)
        for k in range(1, NY):
            total = total + rs_buf[k - 1, n].astype(F32)
        panel_ref[n, own, :] = total.astype(BF)
        whole = panel_ref[n, own, :]
        row = n * 10 * B
        for i in range(4):
            wide = (i + 1) * B
            out = lax.dot_general(whole[:, i * B : wide], whole[:, :wide], TN, preferred_element_type=F32)
            for j in range(i + 1):
                mine[row : row + B, :] = out[:, j * B : j * B + B]
                row += B
        if n == 0:
            start, size = STREAMS[0]
            half = size // 2
            flight = [
                [go(mine.at[rows_at(start + (1 - c) * half, half), :], core_buf.at[pl.ds(start // 2, half), :], twin)]
            ]
    start, size = STREAMS[1]
    half = size // 2
    flight.append(
        [go(mine.at[rows_at(start + (1 - c) * half, half), :], core_buf.at[pl.ds(start // 2, half), :], twin)]
    )

    for s, (start, size) in enumerate(STREAMS):
        half, quarter = size // 2, size // 8
        landed(flight[s])
        here = pl.ds(start // 2, half)
        chip[here, :] = mine[rows_at(start + c * half, half), :] + core_buf[here, :]
        flight[s] = [
            go(
                chip.at[rows_at(start // 2 + ((x + k) % NX) * quarter, quarter), :],
                x_buf.at[k - 1, pl.ds(start // 8, quarter), :],
                near_x[k - 1],
            )
            for k in range(1, NX)
        ]
    for s, (start, size) in enumerate(STREAMS):
        quarter, piece = size // 8, size // 64
        landed(flight[s])
        total = chip[rows_at(start // 2 + x * quarter, quarter), :]
        for k in range(1, NX):
            total = total + x_buf[k - 1, start // 8 : start // 8 + quarter, :]
        x_sum[start // 8 : start // 8 + quarter, :] = total
        flight[s] = [
            go(
                x_sum.at[rows_at(start // 8 + ((z + k) % NZ) * piece, piece), :],
                z_buf.at[k - 1, pl.ds(start // 64, piece), :],
                near_z[k - 1],
            )
            for k in range(1, NZ)
        ]
    for s, (start, size) in enumerate(STREAMS):
        piece = size // 64
        landed(flight[s])
        here = pl.ds(start // 64, piece)
        total = x_sum[rows_at(start // 8 + z * piece, piece), :]
        for k in range(1, NZ):
            total = total + z_buf[k - 1, here, :]
        strip[here, :] = total
        flight[s] = [go(strip.at[here, :], y_buf.at[k - 1, here, :], near_y[k - 1]) for k in range(1, NY)]
    for s, (start, size) in enumerate(STREAMS):
        half, quarter, piece = size // 2, size // 8, size // 64
        landed(flight[s])
        here = pl.ds(start // 64, piece)
        total = strip[here, :]
        for k in range(1, NY):
            total = total + y_buf[k - 1, here, :]
        at = rows_at(start + c * half + x * quarter + z * piece, piece)
        blocks_ref[at, :] = total
        flight[s] = [go(blocks_ref.at[at, :], blocks_ref.at[at, :], peer) for peer in near_z]
    for k in range(1, NY):
        spread.append(go(panel_ref.at[:, own, :], panel_ref.at[:, own, :], near_y[k - 1]))
    launch_near(1)
    combine(1)
    for s, (start, size) in enumerate(STREAMS):
        half, quarter = size // 2, size // 8
        landed(flight[s])
        at = rows_at(start + c * half + x * quarter, quarter)
        flight[s] = [go(blocks_ref.at[at, :], blocks_ref.at[at, :], peer) for peer in near_x]
    for s, (start, size) in enumerate(STREAMS):
        half = size // 2
        landed(flight[s])
        at = rows_at(start + c * half, half)
        flight[s] = [go(blocks_ref.at[at, :], blocks_ref.at[at, :], twin)]
    for copies in flight:
        landed(copies)
    for n in range(LAYERS):
        row = n * 10 * B
        for i in range(4):
            for j in range(i + 1):
                block = blocks_ref[row : row + B, :]
                row += B
                w[n, i * B : i * B + B, j * B : j * B + B] = block
                if i != j:
                    w[n, j * B : j * B + B, i * B : i * B + B] = block.T

    def step(k, carry):
        here = span(k * B, B)
        inv[...] = eliminate(w[:, here, here])
        for at in range(4):

            @pl.when(k == at)
            def _():
                a, z = at * B, at * B + B
                for n in range(LAYERS):
                    inverse = inv[n]
                    right = jnp.dot(inverse, w[n, a:z, :], precision=HIGHEST, preferred_element_type=F32)
                    pieces = [right[:, :a], inverse, right[:, z:]]
                    right = jnp.concatenate([p for p in pieces if p.shape[1]], axis=1)
                    if z < RANK:
                        left = lax.dot_general(
                            w[n, z:, a:z], inverse, NT, precision=HIGHEST, preferred_element_type=F32
                        )
                        w[n, z:, a:z] = jnp.zeros((RANK - z, B), F32)
                        w[n, z:, :] = w[n, z:, :] - jnp.dot(
                            left, right, precision=HIGHEST, preferred_element_type=F32
                        )
                        right = jnp.concatenate([right[:, :z], jnp.zeros((B, RANK - z), F32)], axis=1)
                    w[n, a:z, :] = right

        return carry

    lax.fori_loop(0, 4, step, 0)
    finish_sum(1)
    got = [[go(summed_ref.at[RUNS[r][0], :, cut(1 - c, r)], twin_summed.at[r], twin)] for r in range(len(RUNS))]
    landed(spread)
    for n in range(LAYERS):
        rest = w[n]
        basis = jnp.zeros((ROWS, RANK), F32)
        for _ in range(3):
            part = rest.astype(BF)
            rest = rest - part.astype(F32)
            basis = basis + lax.dot_general(panel_ref[n], part, NT, preferred_element_type=F32)
        basis_ref[n] = basis.astype(BF)
        got[n].append(go(basis_ref.at[n], twin_basis.at[n], twin))
    refs = (first_ref, second_ref, new_first_ref, new_second_ref, delta_ref)
    finish(spot, go, landed, moments, got, refs, (summed_ref, basis_ref, w), tail_scratch)
    for copy in done:
        if id(copy) not in sent:
            copy.wait_send()


def refresh(omega, grads, first, second):
    vmem, hbm = pl.BlockSpec(memory_space=pltpu.VMEM), pl.BlockSpec(memory_space=pltpu.HBM)
    return pl.pallas_call(
        refresh_kernel,
        out_shape=(
            jax.ShapeDtypeStruct((8, LAYERS, OWN), F32),
            jax.ShapeDtypeStruct((8, LAYERS, OWN), F32),
            jax.ShapeDtypeStruct((LAYERS, ROWS, OWN), BF),
        ),
        in_specs=[hbm, hbm, vmem, vmem],
        out_specs=(vmem,) * 3,
        scratch_shapes=[
            pltpu.VMEM((LAYERS, ROWS, OWN), BF),
            pltpu.VMEM((LAYERS, ROWS, RANK), BF),
            pltpu.VMEM((LAYERS, ROWS, RANK), BF),
            pltpu.VMEM((BLOCKS, B), F32),
            pltpu.VMEM((LAYERS, RANK, RANK), F32),
            pltpu.VMEM((LAYERS, B, B), F32),
            pltpu.VMEM((OWN, RANK), BF),
            pltpu.VMEM((NY, LAYERS, ROWS, OWN), BF),
            pltpu.VMEM((FAR, KEPT, RANK), BF),
            pltpu.VMEM((LAYERS, ROWS, OWN - KEPT), BF),
            pltpu.VMEM((LAYERS, ROWS, KEPT), BF),
            pltpu.VMEM((LAYERS, ROWS, OWN - KEPT), BF),
            pltpu.VMEM((LAYERS, ROWS, KEPT), BF),
            pltpu.VMEM((2, LAYERS, ROWS, OWN - KEPT), BF),
            pltpu.VMEM((2, LAYERS, ROWS, KEPT), BF),
            pltpu.VMEM((LAYERS, ROWS, RANK), F32),
            pltpu.VMEM((LAYERS, ROWS, RANK), BF),
            pltpu.VMEM((NY - 1, LAYERS, ROWS // NY, RANK), BF),
            pltpu.VMEM((BLOCKS, B), F32),
            pltpu.VMEM((BLOCKS // 2, B), F32),
            pltpu.VMEM((BLOCKS // 2, B), F32),
            pltpu.VMEM((NX - 1, BLOCKS // 8, B), F32),
            pltpu.VMEM((BLOCKS // 8, B), F32),
            pltpu.VMEM((NZ - 1, BLOCKS // 64, B), F32),
            pltpu.VMEM((BLOCKS // 64, B), F32),
            pltpu.VMEM((NY - 1, BLOCKS // 64, B), F32),
            pltpu.SemaphoreType.DMA((2, 320)),
            pltpu.SemaphoreType.DMA((NY + 1,)),
            pltpu.VMEM((LAYERS, ROWS, RANK), BF),
            pltpu.VMEM((4, ROWS, WIDE), BF),
            pltpu.VMEM((8, LAYERS, HALF), F32),
            pltpu.VMEM((8, LAYERS, HALF), F32),
            pltpu.VMEM((8, LAYERS, HALF), F32),
            pltpu.VMEM((8, LAYERS, HALF), F32),
            pltpu.VMEM((4, 2, B // 2, WIDE), BF),
            pltpu.VMEM((4, 2, B // 2, WIDE), BF),
            pltpu.VMEM((4, 2, B, WIDE), BF),
            pltpu.VMEM((4, 2, B, WIDE), BF),
            pltpu.VMEM((4, B, WIDE), BF),
            pltpu.VMEM((4, NZ - 1, 16, WIDE), BF),
            pltpu.VMEM((4, 16, WIDE), F32),
            pltpu.VMEM((4, 16, WIDE), F32),
            pltpu.VMEM((NC, 4, RANK, WIDE), BF),
        ],
        compiler_params=pltpu.CompilerParams(collective_id=0, has_side_effects=True, vmem_limit_bytes=50 << 20),
    )(omega, grads, first, second)


def local(grad_parts, omega, first_moment, second_moment):
    return refresh(omega, grad_parts[0], first_moment, second_moment)


def solution(mesh):
    return jax.shard_map(
        local,
        mesh=mesh,
        in_specs=(P("dp", None, "mp", None), P("dp", None), P("mp", None, "dp"), P("mp", None, "dp")),
        out_specs=(P("mp", None, "dp"), P("mp", None, "dp"), P(None, "mp", "dp")),
        check_vma=False,
    )
```

```python
import functools

import jax
import jax.numpy as jnp
from jax import lax
from jax.experimental import pallas as pl
from jax.experimental.pallas import tpu as pltpu
from jax.sharding import PartitionSpec as P

HIGHEST = lax.Precision.HIGHEST
MESH = pl.DeviceIdType.MESH
NT = (((1,), (1,)), ((), ()))
TN = (((0,), (0,)), ((), ()))
BF = jnp.bfloat16
F32 = jnp.float32

LAYERS = 2
ROWS = 256
D = 8192
OWN = 2048
HALF = 1024
RANK = 512
B = 128
NY, NX, NZ, NC = 4, 4, 8, 2


def place():
    mp = lax.axis_index("mp")
    return lax.axis_index("dp"), mp // (NZ * NC), (mp // NC) % NZ, mp % NC


def device(y, x, z, c):
    return {"dp": y, "mp": x * (NZ * NC) + z * NC + c}


def greet(peers):
    barrier = pltpu.get_barrier_semaphore()
    for peer in peers:
        pl.semaphore_signal(barrier, inc=1, device_id=peer, device_id_type=MESH)
    pl.semaphore_wait(barrier, len(peers))


def along(axis, spot, k):
    y, x, z, c = spot
    if axis == "y":
        return device((y + k) % NY, x, z, c)
    if axis == "x":
        return device(y, (x + k) % NX, z, c)
    if axis == "z":
        return device(y, x, (z + k) % NZ, c)
    return device(y, x, z, 1 - c)


def ship(src, dst, send, recv, peer):
    copy = pltpu.make_async_remote_copy(
        src_ref=src, dst_ref=dst, send_sem=send, recv_sem=recv, device_id=peer, device_id_type=MESH
    )
    copy.start()
    return copy


def span(start, size):
    return pl.ds(pl.multiple_of(start, size), size)


RUNS = ((0, 0), (1, 0), (0, 512), (1, 512))
WIDE = 512


def cut(core, r):
    return pl.ds(pl.multiple_of(core * HALF + RUNS[r][1], WIDE), WIDE)


def finish(spot, go, landed, moments, got, refs, held, scratch):
    y, x, z, c = spot
    first_ref, second_ref, new_first_ref, new_second_ref, delta_ref = refs
    summed_ref, basis_ref, x_own = held
    (
        twin_basis,
        twin_summed,
        twin_first,
        twin_second,
        back_first,
        back_second,
        relay_out,
        relay_in,
        near_out,
        near_in,
        z_out,
        z_in,
        z_own,
        joined,
        gathered,
    ) = scratch
    twin = along("c", spot, 1)
    up, down = along("x", spot, 1), along("x", spot, NX - 1)
    near_z = [along("z", spot, k) for k in range(1, NZ)]
    mine = span(c * HALF, HALF)

    def product(r, start, size):
        here, n = span(start, size), RUNS[r][0]
        out = lax.dot_general(basis_ref[n, :, here], summed_ref[n, :, cut(c, r)], TN, preferred_element_type=F32)
        return out + lax.dot_general(twin_basis[n, :, here], twin_summed[r], TN, preferred_element_type=F32)

    h = B // 2
    above, below, across = ((x + 1) % NX) * B, ((x + NX - 1) % NX) * B, ((x + 2) % NX) * B
    relays, nears, spreads, firsts, seconds = {}, {}, {}, {}, {}
    z_copies, crossed = {}, {}
    slot = span(x * B + z * 16, 16)
    ours, theirs = span(c * 8, 8), span((1 - c) * 8, 8)

    def part(n, start, size):
        return gathered.at[c, n, pl.ds(pl.multiple_of(start, size), size), :]

    def kept(n, start, size):
        return slice((n % 2) * 2 * B + start, (n % 2) * 2 * B + start + size)

    def multiply(n):
        landed(got[n])
        far = product(n, across, B)
        relay_out[n, 0] = far[:h].astype(BF)
        relay_out[n, 1] = far[h:].astype(BF)
        relays[n] = [go(relay_out.at[n, 0], relay_in.at[n, 0], up), go(relay_out.at[n, 1], relay_in.at[n, 1], down)]
        out = product(n, above, B)
        x_own[n // 2, kept(n, B, h), :] = out[:h]
        near_out[n, 0, h:, :] = out[h:].astype(BF)
        nears[n] = [go(near_out.at[n, 0, pl.ds(h, h), :], near_in.at[n, 0, pl.ds(h, h), :], up)]
        out = product(n, below, B)
        x_own[n // 2, kept(n, B + h, h), :] = out[h:]
        near_out[n, 1, :h, :] = out[:h].astype(BF)
        nears[n].append(go(near_out.at[n, 1, pl.ds(0, h), :], near_in.at[n, 1, pl.ds(0, h), :], down))
        x_own[n // 2, kept(n, 0, B), :] = product(n, x * B, B)

    def pass_on(n):
        relays[n][0].wait_recv()
        near_out[n, 0, :h, :] = (x_own[n // 2, kept(n, B, h), :] + relay_in[n, 0].astype(F32)).astype(BF)
        nears[n].append(go(near_out.at[n, 0, pl.ds(0, h), :], near_in.at[n, 0, pl.ds(0, h), :], up))
        relays[n][1].wait_recv()
        near_out[n, 1, h:, :] = (x_own[n // 2, kept(n, B + h, h), :] + relay_in[n, 1].astype(F32)).astype(BF)
        nears[n].append(go(near_out.at[n, 1, pl.ds(h, h), :], near_in.at[n, 1, pl.ds(h, h), :], down))

    def over_z(n):
        landed(nears[n])
        total = x_own[n // 2, kept(n, 0, B), :] + near_in[n, 0].astype(F32) + near_in[n, 1].astype(F32)
        x_own[n // 2, kept(n, 0, B), :] = total
        z_out[n] = total.astype(BF)
        z_copies[n] = [
            go(z_out.at[n, span(((z + k) % NZ) * 16, 16), :], z_in.at[n, k - 1], near_z[k - 1]) for k in range(1, NZ)
        ]

    def adam(projected, first, second):
        new_first = 0.9 * first + 0.1 * projected
        new_second = 0.999 * second + 0.001 * projected * projected
        return new_first, new_second, new_first / (jnp.sqrt(new_second) + 1e-08)

    def update(n):
        layer, off = RUNS[n]
        here, there = cut(c, n), pl.ds(off, WIDE)
        if n == 0:
            landed(moments)
        landed(z_copies[n])
        total = x_own[n // 2, pl.ds(pl.multiple_of((n % 2) * 2 * B + z * 16, 16), 16), :]
        for k in range(1, NZ):
            total = total + z_in[n, k - 1].astype(F32)
        z_own[n] = total
        new_first, new_second, fresh = adam(z_own[n, ours, :], first_ref[:, layer, here], second_ref[:, layer, here])
        new_first_ref[:, layer, here] = new_first
        new_second_ref[:, layer, here] = new_second
        joined[n, ours, :] = fresh
        new_first, new_second, fresh = adam(z_own[n, theirs, :], twin_first[:, layer, there], twin_second[:, layer, there])
        back_first[:, layer, there] = new_first
        back_second[:, layer, there] = new_second
        joined[n, theirs, :] = fresh
        gathered[c, n, slot, :] = joined[n].astype(BF)
        piece = gathered.at[c, n, slot, :]
        spreads[n] = [go(piece, piece, peer) for peer in near_z]

    def over_x(n):
        landed(spreads[n])
        low, high, whole = part(n, x * B, h), part(n, x * B + h, h), part(n, x * B, B)
        firsts[n] = [go(low, low, up), go(high, high, down), go(high, high, up), go(low, low, down)]
        crossed[n] = [go(whole, whole, twin)]

    def forward(n):
        firsts[n][0].wait_recv()
        low = part(n, below, h)
        seconds[n] = [go(low, low, up)]
        firsts[n][1].wait_recv()
        high = part(n, above + h, h)
        seconds[n].append(go(high, high, down))
        landed(firsts[n][2:])
        for start in (below, above):
            whole = part(n, start, B)
            crossed[n].append(go(whole, whole, twin))

    def cross(n):
        landed(seconds[n])
        whole = part(n, across, B)
        crossed[n].append(go(whole, whole, twin))

    def apply(n):
        layer, off = RUNS[n]
        landed(crossed[n])
        for core in range(NC):
            out = jnp.dot(basis_ref[layer], gathered[core, n], preferred_element_type=F32)
            delta_ref[layer, :, core * HALF + off : core * HALF + off + WIDE] = out.astype(BF)

    stages = (multiply, pass_on, over_z, update, over_x, forward, cross, apply)
    for tick in range(len(RUNS) + len(stages) - 1):
        for lag, stage in enumerate(stages):
            if 0 <= tick - lag < len(RUNS):
                stage(tick - lag)
    backs = [
        go(back_first, new_first_ref.at[:, :, mine], twin),
        go(back_second, new_second_ref.at[:, :, mine], twin),
    ]
    landed(backs)


def eliminate(whole):
    lane = lax.broadcasted_iota(jnp.int32, (1, 8, B), 2)
    sub = lax.broadcasted_iota(jnp.int32, (1, 8, B), 1)
    sub4 = lax.broadcasted_iota(jnp.int32, (1, 1, 8, B), 2)
    found = []
    for b in range(B // 8):
        inside = (lane >= 8 * b) & (lane < 8 * b + 8)
        top = whole[:, :8, :]
        cols = [top[:, :, 8 * b + k : 8 * b + k + 1] for k in range(8)]
        cols = jnp.stack([jnp.broadcast_to(col, (LAYERS, 8, B)) for col in cols], axis=1)
        start = jnp.where(inside, (lane == sub + 8 * b).astype(F32), top)
        state = jnp.concatenate([cols, start[:, None]], axis=1)
        forward = start
        scale = jnp.zeros((LAYERS, 8, B), F32)
        for k in range(8):
            column = state[:, k]
            pivot = column[:, k : k + 1, :]
            inverse = 1.0 / pivot
            factor = column * inverse
            line = state[:, :, k : k + 1, :]
            state = jnp.where(sub4 == k, line * inverse[:, None], state - factor[:, None] * line)
            forward = jnp.where(sub > k, forward - factor * forward[:, k : k + 1, :], forward)
            scale = jnp.where(sub == k, pivot, scale)
        found.append(jnp.where(lane < 8 * b + 8, forward, 0.0) * lax.rsqrt(scale))
        if b < B // 8 - 1:
            rest = whole[:, 8:, :]
            total = None
            for k in range(8):
                term = rest[:, :, 8 * b + k : 8 * b + k + 1] * state[:, 8, k : k + 1, :]
                total = term if total is None else total + term
            whole = jnp.where(inside[:, :1], 0.0, rest) - total
    return jnp.concatenate(found, axis=1)


STREAMS = ((0, 1024), (1024, 1536))
BLOCKS = LAYERS * 10 * B
FAR = NY - 1
SPLIT, EXTRA = 1024, 256
KEPT = SPLIT + EXTRA
PARTS = ((KEPT, OWN - KEPT), (0, KEPT))


def rows_at(start, size):
    return pl.ds(pl.multiple_of(start, 8), size)


def refresh_kernel(
    omega_hbm,
    grads_hbm,
    first_ref,
    second_ref,
    new_first_ref,
    new_second_ref,
    delta_ref,
    summed_ref,
    basis_ref,
    panel_ref,
    blocks_ref,
    w,
    inv,
    omega_ref,
    grads,
    omegas,
    relay_a,
    relay_b,
    joint_a,
    joint_b,
    near_a,
    near_b,
    partial,
    part,
    rs_buf,
    mine,
    core_buf,
    chip,
    x_buf,
    x_sum,
    z_buf,
    strip,
    y_buf,
    sems,
    local_sems,
    *tail_scratch,
):
    spot = place()
    y, x, z, c = spot
    twin = along("c", spot, 1)
    near_y = [along("y", spot, k) for k in range(1, NY)]
    near_x = [along("x", spot, k) for k in range(1, NX)]
    near_z = [along("z", spot, k) for k in range(1, NZ)]
    loads = [pltpu.make_async_copy(omega_hbm, omega_ref, local_sems.at[NY])]
    loads[0].start()
    for k in (0, 1, 3, 2):
        columns = span(((y + k) % NY) * OWN, OWN)
        load = pltpu.make_async_copy(grads_hbm.at[:, :, columns], grads.at[k], local_sems.at[k])
        load.start()
        loads.append(load)
    greet([twin] + near_y + near_x + near_z)
    done, sent = [], []
    count = [0]

    def go(src, dst, peer):
        copy = ship(src, dst, sems.at[0, count[0]], sems.at[1, count[0]], peer)
        count[0] += 1
        done.append(copy)
        return copy

    def landed(copies):
        for copy in copies:
            copy.wait_recv()

    twin_basis, twin_summed, twin_first, twin_second = tail_scratch[:4]
    other = span((1 - c) * HALF, HALF)
    relay_in, joint, near_in = (relay_a, relay_b), (joint_a, joint_b), (near_a, near_b)
    relays, nears = [None] * 2, [None] * 2

    SUB = ROWS // 2

    def columns(part_of, k):
        off, width = PARTS[part_of]
        return pl.ds(pl.multiple_of(((y + k) % NY) * OWN + off, 2 * B), width)

    def launch(part_of):
        relays[part_of] = [
            [
                go(
                    grads_hbm.at[n, pl.ds(r * SUB, SUB), columns(part_of, 2)],
                    relay_in[part_of].at[n, pl.ds(r * SUB, SUB), :],
                    near_y[2 * n],
                )
                for n in range(2)
            ]
            for r in range(2)
        ]

    def launch_near(part_of):
        for copies in relays[part_of]:
            for copy in copies:
                copy.wait_send()
                sent.append(id(copy))
        nears[part_of] = [
            go(grads_hbm.at[1, :, columns(part_of, 1)], near_in[part_of].at[0, 1], near_y[0]),
            go(grads_hbm.at[0, :, columns(part_of, 3)], near_in[part_of].at[1, 0], near_y[2]),
        ]

    def in_rows(first_row, count_rows, work):
        def body(t, carry):
            work(pl.ds(pl.multiple_of(first_row + t * 32, 32), 32))
            return carry

        lax.fori_loop(0, count_rows // 32, body, 0)

    def combine(part_of):
        off, width = PARTS[part_of]
        for r in range(2):
            for n, k in ((0, 1), (1, 3)):
                relays[part_of][r][n].wait_recv()

                def work(at):
                    own_term = grads[k, n, at, off : off + width].astype(F32)
                    joint[part_of][n, at, :] = (own_term + relay_in[part_of][n, at, :].astype(F32)).astype(BF)

                in_rows(r * SUB, SUB, work)
                at = pl.ds(r * SUB, SUB)
                nears[part_of].append(
                    go(joint[part_of].at[n, at, :], near_in[part_of].at[n, n, at, :], near_y[k - 1])
                )

    def finish_sum(part_of):
        off, width = PARTS[part_of]
        landed(nears[part_of])

        def work(at):
            for n in range(LAYERS):
                out = grads[0, n, at, off : off + width].astype(F32) + near_in[part_of][0, n, at, :].astype(F32)
                summed_ref[n, at, off : off + width] = (out + near_in[part_of][1, n, at, :].astype(F32)).astype(BF)

        in_rows(0, ROWS, work)

    strip_at = span(x * 256 + c * B + z * 16, 16)
    slices = [go(omega_hbm.at[strip_at, :], omegas.at[FAR - k, strip_at, :], near_y[k - 1]) for k in range(1, NY)]
    extra_at = rows_at(SPLIT + c * B + z * 16, 16)
    extras = [go(omega_hbm.at[extra_at, :], omegas.at[FAR - k, extra_at, :], near_y[k - 1]) for k in range(1, NY)]
    launch(0)
    moments = [
        go(first_ref.at[:, :, other], twin_first, twin),
        go(second_ref.at[:, :, other], twin_second, twin),
    ]

    def block(s, which, start, size):
        return omegas.at[s, pl.ds(pl.multiple_of(which * 256 + c * B + start, size), size), :]

    flights = []
    for s in range(FAR):
        slices[FAR - 1 - s].wait_recv()
        piece = omegas.at[s, strip_at, :]
        flights.append([go(piece, piece, peer) for peer in near_z])
    landed(extras)
    piece = omegas.at[:, extra_at, :]
    extras = [go(piece, piece, peer) for peer in near_z]
    for load in loads:
        load.wait()
    for n in range(LAYERS):
        partial[n] = jnp.dot(grads[0, n, :, :KEPT], omega_ref[:KEPT, :], preferred_element_type=F32)
    launch_near(0)
    up, down = near_x[0], near_x[2]
    above, below, across = (x + 1) % NX, (x + NX - 1) % NX, (x + 2) % NX
    h = B // 2
    firsts, crossed, seconds = [], [], []
    for s in range(FAR):
        landed(flights[s])
        low, high, whole = block(s, x, 0, h), block(s, x, h, h), block(s, x, 0, B)
        firsts.append([go(low, low, up), go(high, high, down), go(high, high, up), go(low, low, down)])
        crossed.append([go(whole, whole, twin)])
    combine(0)
    for s in range(FAR):
        firsts[s][0].wait_recv()
        low = block(s, below, 0, h)
        seconds.append([go(low, low, up)])
        firsts[s][1].wait_recv()
        high = block(s, above, h, h)
        seconds[s].append(go(high, high, down))
        landed(firsts[s][2:])
        for which in (below, above):
            whole = block(s, which, 0, B)
            crossed[s].append(go(whole, whole, twin))
    landed(extras)
    piece = omegas.at[:, rows_at(SPLIT + c * B, B), :]
    crossed[0].append(go(piece, piece, twin))
    for s in range(FAR):
        landed(seconds[s])
        whole = block(s, across, 0, B)
        crossed[s].append(go(whole, whole, twin))
    for s in range(FAR):
        landed(crossed[s])
        for n in range(LAYERS):
            partial[n] += jnp.dot(grads[s + 1, n, :, :KEPT], omegas[s], preferred_element_type=F32)
    finish_sum(0)
    for n in range(LAYERS):
        out = partial[n] + jnp.dot(summed_ref[n, :, KEPT:], omega_ref[KEPT:, :], preferred_element_type=F32)
        part[n] = out.astype(BF)

    q = ROWS // NY
    own = span(y * q, q)
    first = [
        [
            go(part.at[n, span(((y + k) % NY) * q, q), :], rs_buf.at[k - 1, n], near_y[k - 1])
            for k in range(1, NY)
        ]
        for n in range(LAYERS)
    ]
    spread = []
    for n in range(LAYERS):
        landed(first[n])
        if n == 1:
            launch(1)
        total = part[n, own, :].astype(F32)
        for k in range(1, NY):
            total = total + rs_buf[k - 1, n].astype(F32)
        panel_ref[n, own, :] = total.astype(BF)
        whole = panel_ref[n, own, :]
        row = n * 10 * B
        for i in range(4):
            wide = (i + 1) * B
            out = lax.dot_general(whole[:, i * B : wide], whole[:, :wide], TN, preferred_element_type=F32)
            for j in range(i + 1):
                mine[row : row + B, :] = out[:, j * B : j * B + B]
                row += B
        if n == 0:
            start, size = STREAMS[0]
            half = size // 2
            flight = [
                [go(mine.at[rows_at(start + (1 - c) * half, half), :], core_buf.at[pl.ds(start // 2, half), :], twin)]
            ]
    start, size = STREAMS[1]
    half = size // 2
    flight.append(
        [go(mine.at[rows_at(start + (1 - c) * half, half), :], core_buf.at[pl.ds(start // 2, half), :], twin)]
    )

    for s, (start, size) in enumerate(STREAMS):
        half, quarter = size // 2, size // 8
        landed(flight[s])
        here = pl.ds(start // 2, half)
        chip[here, :] = mine[rows_at(start + c * half, half), :] + core_buf[here, :]
        flight[s] = [
            go(
                chip.at[rows_at(start // 2 + ((x + k) % NX) * quarter, quarter), :],
                x_buf.at[k - 1, pl.ds(start // 8, quarter), :],
                near_x[k - 1],
            )
            for k in range(1, NX)
        ]
    for s, (start, size) in enumerate(STREAMS):
        quarter, piece = size // 8, size // 64
        landed(flight[s])
        total = chip[rows_at(start // 2 + x * quarter, quarter), :]
        for k in range(1, NX):
            total = total + x_buf[k - 1, start // 8 : start // 8 + quarter, :]
        x_sum[start // 8 : start // 8 + quarter, :] = total
        flight[s] = [
            go(
                x_sum.at[rows_at(start // 8 + ((z + k) % NZ) * piece, piece), :],
                z_buf.at[k - 1, pl.ds(start // 64, piece), :],
                near_z[k - 1],
            )
            for k in range(1, NZ)
        ]
    for s, (start, size) in enumerate(STREAMS):
        piece = size // 64
        landed(flight[s])
        here = pl.ds(start // 64, piece)
        total = x_sum[rows_at(start // 8 + z * piece, piece), :]
        for k in range(1, NZ):
            total = total + z_buf[k - 1, here, :]
        strip[here, :] = total
        flight[s] = [go(strip.at[here, :], y_buf.at[k - 1, here, :], near_y[k - 1]) for k in range(1, NY)]
    for s, (start, size) in enumerate(STREAMS):
        half, quarter, piece = size // 2, size // 8, size // 64
        landed(flight[s])
        here = pl.ds(start // 64, piece)
        total = strip[here, :]
        for k in range(1, NY):
            total = total + y_buf[k - 1, here, :]
        at = rows_at(start + c * half + x * quarter + z * piece, piece)
        blocks_ref[at, :] = total
        flight[s] = [go(blocks_ref.at[at, :], blocks_ref.at[at, :], peer) for peer in near_z]
    for k in range(1, NY):
        spread.append(go(panel_ref.at[:, own, :], panel_ref.at[:, own, :], near_y[k - 1]))
    launch_near(1)
    combine(1)
    for s, (start, size) in enumerate(STREAMS):
        half, quarter = size // 2, size // 8
        landed(flight[s])
        at = rows_at(start + c * half + x * quarter, quarter)
        flight[s] = [go(blocks_ref.at[at, :], blocks_ref.at[at, :], peer) for peer in near_x]
    for s, (start, size) in enumerate(STREAMS):
        half = size // 2
        landed(flight[s])
        at = rows_at(start + c * half, half)
        flight[s] = [go(blocks_ref.at[at, :], blocks_ref.at[at, :], twin)]
    for copies in flight:
        landed(copies)
    for n in range(LAYERS):
        row = n * 10 * B
        for i in range(4):
            for j in range(i + 1):
                block = blocks_ref[row : row + B, :]
                row += B
                w[n, i * B : i * B + B, j * B : j * B + B] = block
                if i != j:
                    w[n, j * B : j * B + B, i * B : i * B + B] = block.T

    def step(k, carry):
        here = span(k * B, B)
        inv[...] = eliminate(w[:, here, here])
        for at in range(4):

            @pl.when(k == at)
            def _():
                a, z = at * B, at * B + B
                for n in range(LAYERS):
                    inverse = inv[n]
                    right = jnp.dot(inverse, w[n, a:z, :], precision=HIGHEST, preferred_element_type=F32)
                    pieces = [right[:, :a], inverse, right[:, z:]]
                    right = jnp.concatenate([p for p in pieces if p.shape[1]], axis=1)
                    if z < RANK:
                        left = lax.dot_general(
                            w[n, z:, a:z], inverse, NT, precision=HIGHEST, preferred_element_type=F32
                        )
                        w[n, z:, a:z] = jnp.zeros((RANK - z, B), F32)
                        w[n, z:, :] = w[n, z:, :] - jnp.dot(
                            left, right, precision=HIGHEST, preferred_element_type=F32
                        )
                        right = jnp.concatenate([right[:, :z], jnp.zeros((B, RANK - z), F32)], axis=1)
                    w[n, a:z, :] = right

        return carry

    lax.fori_loop(0, 4, step, 0)
    finish_sum(1)
    got = [[go(summed_ref.at[RUNS[r][0], :, cut(1 - c, r)], twin_summed.at[r], twin)] for r in range(len(RUNS))]
    landed(spread)
    for n in range(LAYERS):
        rest = w[n]
        basis = jnp.zeros((ROWS, RANK), F32)
        for _ in range(3):
            part = rest.astype(BF)
            rest = rest - part.astype(F32)
            basis = basis + lax.dot_general(panel_ref[n], part, NT, preferred_element_type=F32)
        basis_ref[n] = basis.astype(BF)
        got[n].append(go(basis_ref.at[n], twin_basis.at[n], twin))
    refs = (first_ref, second_ref, new_first_ref, new_second_ref, delta_ref)
    finish(spot, go, landed, moments, got, refs, (summed_ref, basis_ref, w), tail_scratch)
    for copy in done:
        if id(copy) not in sent:
            copy.wait_send()


def refresh(omega, grads, first, second):
    vmem, hbm = pl.BlockSpec(memory_space=pltpu.VMEM), pl.BlockSpec(memory_space=pltpu.HBM)
    return pl.pallas_call(
        refresh_kernel,
        out_shape=(
            jax.ShapeDtypeStruct((8, LAYERS, OWN), F32),
            jax.ShapeDtypeStruct((8, LAYERS, OWN), F32),
            jax.ShapeDtypeStruct((LAYERS, ROWS, OWN), BF),
        ),
        in_specs=[hbm, hbm, vmem, vmem],
        out_specs=(vmem,) * 3,
        scratch_shapes=[
            pltpu.VMEM((LAYERS, ROWS, OWN), BF),
            pltpu.VMEM((LAYERS, ROWS, RANK), BF),
            pltpu.VMEM((LAYERS, ROWS, RANK), BF),
            pltpu.VMEM((BLOCKS, B), F32),
            pltpu.VMEM((LAYERS, RANK, RANK), F32),
            pltpu.VMEM((LAYERS, B, B), F32),
            pltpu.VMEM((OWN, RANK), BF),
            pltpu.VMEM((NY, LAYERS, ROWS, OWN), BF),
            pltpu.VMEM((FAR, KEPT, RANK), BF),
            pltpu.VMEM((LAYERS, ROWS, OWN - KEPT), BF),
            pltpu.VMEM((LAYERS, ROWS, KEPT), BF),
            pltpu.VMEM((LAYERS, ROWS, OWN - KEPT), BF),
            pltpu.VMEM((LAYERS, ROWS, KEPT), BF),
            pltpu.VMEM((2, LAYERS, ROWS, OWN - KEPT), BF),
            pltpu.VMEM((2, LAYERS, ROWS, KEPT), BF),
            pltpu.VMEM((LAYERS, ROWS, RANK), F32),
            pltpu.VMEM((LAYERS, ROWS, RANK), BF),
            pltpu.VMEM((NY - 1, LAYERS, ROWS // NY, RANK), BF),
            pltpu.VMEM((BLOCKS, B), F32),
            pltpu.VMEM((BLOCKS // 2, B), F32),
            pltpu.VMEM((BLOCKS // 2, B), F32),
            pltpu.VMEM((NX - 1, BLOCKS // 8, B), F32),
            pltpu.VMEM((BLOCKS // 8, B), F32),
            pltpu.VMEM((NZ - 1, BLOCKS // 64, B), F32),
            pltpu.VMEM((BLOCKS // 64, B), F32),
            pltpu.VMEM((NY - 1, BLOCKS // 64, B), F32),
            pltpu.SemaphoreType.DMA((2, 320)),
            pltpu.SemaphoreType.DMA((NY + 1,)),
            pltpu.VMEM((LAYERS, ROWS, RANK), BF),
            pltpu.VMEM((4, ROWS, WIDE), BF),
            pltpu.VMEM((8, LAYERS, HALF), F32),
            pltpu.VMEM((8, LAYERS, HALF), F32),
            pltpu.VMEM((8, LAYERS, HALF), F32),
            pltpu.VMEM((8, LAYERS, HALF), F32),
            pltpu.VMEM((4, 2, B // 2, WIDE), BF),
            pltpu.VMEM((4, 2, B // 2, WIDE), BF),
            pltpu.VMEM((4, 2, B, WIDE), BF),
            pltpu.VMEM((4, 2, B, WIDE), BF),
            pltpu.VMEM((4, B, WIDE), BF),
            pltpu.VMEM((4, NZ - 1, 16, WIDE), BF),
            pltpu.VMEM((4, 16, WIDE), F32),
            pltpu.VMEM((4, 16, WIDE), F32),
            pltpu.VMEM((NC, 4, RANK, WIDE), BF),
        ],
        compiler_params=pltpu.CompilerParams(collective_id=0, has_side_effects=True, vmem_limit_bytes=50 << 20),
    )(omega, grads, first, second)


def store_kernel(*refs):
    sources, targets, sems = refs[:3], refs[3:6], refs[6]
    copies = [pltpu.make_async_copy(sources[i], targets[i], sems.at[i]) for i in range(3)]
    for copy in copies:
        copy.start()
    for copy in copies:
        copy.wait()


def store(*results):
    anywhere = pl.BlockSpec(memory_space=pl.ANY)
    return pl.pallas_call(
        store_kernel,
        out_shape=tuple(jax.ShapeDtypeStruct(r.shape, r.dtype) for r in results),
        in_specs=[pl.BlockSpec(memory_space=pltpu.VMEM)] * 3,
        out_specs=(anywhere,) * 3,
        scratch_shapes=[pltpu.SemaphoreType.DMA((3,))],
    )(*results)


def local(grad_parts, omega, first_moment, second_moment):
    return store(*refresh(omega, grad_parts[0], first_moment, second_moment))


def solution(mesh):
    return jax.shard_map(
        local,
        mesh=mesh,
        in_specs=(P("dp", None, "mp", None), P("dp", None), P("mp", None, "dp"), P("mp", None, "dp")),
        out_specs=(P("mp", None, "dp"), P("mp", None, "dp"), P(None, "mp", "dp")),
        check_vma=False,
    )
```
